256 devices in a mesh: req: 64 (over z, y, core), tp: 4 (over x).
Axes of the slice: x: 4, y: 4, z: 8, core: 2. Of those that a mesh axis runs over, the one named last changes fastest.
Arguments:
- projected: bfloat16 [8448, 3, 2048], P('req', None, 'tp'), may hold values from -400 to 400
- residual: bfloat16 [8448, 2048], P('req'), may hold values from -8 to 8
- query_gain: float32 [2048], P('tp'), may hold values from 0.6 to 2
- key_gain: float32 [2048], P('tp'), may hold values from 0.6 to 2
- context_cache: bfloat16 [64, 512, 2, 2048], P('req', None, None, 'tp'), may hold values from -6 to 6
- decode_cache: bfloat16 [256, 512, 2, 2048], P('req', None, None, 'tp'), may hold values from -6 to 6
- offsets: int32 [64], P('req'), may hold values from 0 to 512, as said below
- lengths: int32 [256], P('req'), may hold values from 1 to 512, as said below
- group_order: int32 [64], replicated, may hold values from 0 to 63, each once
- expert_ids: int32 [8448, 8], P('req'), may hold values from 0 to 63, all different within a row; in each aligned block of 132 rows (0 to 131, 132 to 263, ...) at most 32 rows name the same one
- out_weight: bfloat16 [2048, 2048], P('tp'), may hold values from -0.125 to 0.125
- post_gain: float32 [2048], replicated, may hold values from 0.25 to 1.75
- router: bfloat16 [2048, 64], replicated, may hold values from -12 to 12
- gate_weight: bfloat16 [64, 2048, 1024], P('req', None, 'tp'), may hold values from -0.125 to 0.125
- up_weight: bfloat16 [64, 2048, 1024], P('req', None, 'tp'), may hold values from -0.125 to 0.125
- down_weight: bfloat16 [64, 1024, 2048], P('req', 'tp'), may hold values from -0.1875 to 0.1875
Outputs:
- out: bfloat16 [8448, 2048], P('req', 'tp')
The draws below stay inside these ranges and needn't reach their ends.
Inputs may be any that keep to these rules, and one draw needn't show every extreme that they name: `offsets`: some group has exactly 512 cached tokens. `lengths`: some decode request has exactly 512 cached tokens. `group_order`: each group index appears once. `expert_ids`: each token names 8 different experts. Among the 132 rows of one device no expert is named more than 32 times, and some device's rows name one expert exactly 32 times.
All inputs are finite; a program needn't handle non-finite values.
Results may differ from the reference program's by a relative error of at most 0.02.
The reference program's roundings to bfloat16 on the way count: a program that leaves them out, or rounds other values in their place, can miss the bound.
Values may be sent and summed in bfloat16 or wider, within the bound.
No kernel may reach another device: no remote copies, remote signals or barrier semaphores. Data moves between devices by JAX's collectives and lax.ppermute only.
A program may use at most 128 MiB of HBM per device.

```python
import math
import jax
import jax.numpy as jnp
import numpy as np
from jax import lax

D = 2048
HEADS = 16
HEAD_DIM = 128
EXP_FF = 1024
TOPK = 8
PRE_TOK = 128
DEC_DEV = 4
CONTEXT = 512
CACHE = 512
EXPERTS = 64
GROUPS = 64
ROWS = 132
TOKENS = 8448
DECODES = 256
CAP = 32
N_TP = 4


def column_rise(span):
    column = jnp.arange(D, dtype=jnp.float32)
    return span ** (jnp.floor(column / HEAD_DIM) / max(HEADS - 1, 1))


def draw_projected(key, part):
    keys_all = jax.random.split(jax.random.fold_in(key, 101), 3)
    rows_scale = 10.0 ** jax.random.uniform(keys_all[1], (TOKENS, 1, 1), jnp.float32)
    roughness = 2.0 ** jax.random.uniform(keys_all[2], (1, 3, D), jnp.float32, -1.0, 1.0)
    which_part = jnp.arange(3)[None, :, None]
    samples = jax.random.normal(keys_all[0], (TOKENS, 3, D), jnp.float32)
    scaled = jnp.where(which_part < 2, samples * rows_scale * column_rise(3.0)[None, None, :] * roughness, samples)
    return jnp.clip(scaled, -400.0, 400.0).astype(jnp.bfloat16)


def draw_residual(key, part):
    keys_all = jax.random.split(jax.random.fold_in(key, 202), 3)
    rows_scale = 10.0 ** jax.random.uniform(keys_all[1], (TOKENS, 1), jnp.float32, -0.5, 0.5)
    column = jnp.arange(D, dtype=jnp.float32)
    roughness = 2.0 ** jax.random.uniform(keys_all[2], (1, D), jnp.float32, -0.5, 0.5)
    samples = jax.random.normal(keys_all[0], (TOKENS, D), jnp.float32)
    rising = 3.0 ** (column / (D - 1)) / 1.7
    return jnp.clip(0.1 * samples * rows_scale * rising[None, :] * roughness, -8.0, 8.0).astype(jnp.bfloat16)


def draw_query_gain(key, part):
    folded = jax.random.fold_in(key, 303)
    return jax.random.uniform(folded, (D,), jnp.float32, 0.6, 1.4)


def draw_key_gain(key, part):
    folded = jax.random.fold_in(key, 404)
    return jax.random.uniform(folded, (D,), jnp.float32, 0.6, 1.4)


def draw_router(key, part):
    first_key = jax.random.fold_in(jax.random.fold_in(key, 505), 0)
    samples = jax.random.normal(first_key, (D, EXPERTS), jnp.float32)
    return jnp.clip(samples * (0.2 / math.sqrt(D)), -12.0, 12.0).astype(jnp.bfloat16)


def draw_offsets(key, part):
    first_key, second_key = jax.random.split(jax.random.fold_in(key, 606))
    sampled = jax.random.randint(first_key, (GROUPS,), 0, CONTEXT + 1)
    chosen = jax.random.randint(second_key, (), 0, GROUPS)
    return jnp.where(jnp.arange(GROUPS) == chosen, CONTEXT, sampled).astype(jnp.int32)


def draw_lengths(key, part):
    keys_all = jax.random.split(jax.random.fold_in(key, 707), 3)
    halvings = jax.random.randint(keys_all[0], (DECODES,), 0, 6)
    ceiling = jnp.maximum(CACHE // jnp.left_shift(1, halvings), 1)
    spread = jax.random.randint(keys_all[1], (DECODES,), 0, 1 << 20) % (ceiling - ceiling // 2 + 1)
    sampled = jnp.maximum(ceiling // 2 + spread, 1)
    chosen = jax.random.randint(keys_all[2], (), 0, DECODES)
    return jnp.where(jnp.arange(DECODES) == chosen, CACHE, sampled).astype(jnp.int32)


def shard_levels(rng, extent, cuts, low, high):
    def one(position, blocks):
        draws = jax.random.uniform(jax.random.fold_in(jax.random.fold_in(rng, 6), position), (blocks,), jnp.float32, low / len(cuts), high / len(cuts))
        return jnp.repeat(jnp.exp(draws), extent[position] // blocks).reshape((-1,) + (1,) * (len(extent) - position - 1))

    factor_of = one(*cuts[0])
    for cut in cuts[1:]:
        factor_of = factor_of * one(*cut)
    return factor_of


def shared_out(rng, own, number, rows, count, top, most, skew):
    ranking = jax.random.permutation(rng, count)
    packed, usual = portions_of(count, rows * top, most, skew, True), portions_of(count, rows * top, most, skew, False)
    places = jnp.arange(count)

    def named(sizes, offset_by):
        used = int((sizes > 0).sum())
        fixed = max(1, used // 4)
        passed = fixed + (places - fixed + offset_by * (used - fixed)) % max(1, count - fixed)
        return jnp.zeros((count,), jnp.int32).at[ranking[jnp.where(places < fixed, places, passed)]].set(jnp.asarray(sizes, jnp.int32))

    sizes = jnp.where(number % 4 == 0, named(packed, number // 4), named(usual, number - number // 4 - 1))
    mixed = jax.random.permutation(jax.random.fold_in(own, 3), count)
    source_of, taker = mixed[0:count // 2 * 2:2], mixed[1:count // 2 * 2:2]
    room = jnp.minimum(sizes[source_of] - 1, most - sizes[taker]) // 2
    room = jnp.where((source_of == ranking[0]) | (taker == ranking[0]) | (sizes[taker] == 0), 0, jnp.maximum(room, 0))
    passed = jax.random.randint(jax.random.fold_in(own, 4), (count // 2,), 0, 1 << 20) % (room + 1)
    sizes = sizes.at[source_of].add(-passed).at[taker].add(passed)
    items = jnp.searchsorted(jnp.cumsum(sizes), jnp.arange(rows * top), side="right").astype(jnp.int32)
    listing = items.reshape(top, rows).T
    listing = listing[jax.random.permutation(jax.random.fold_in(own, 1), rows)]
    offset_by = jax.random.randint(jax.random.fold_in(own, 2), (rows, 1), 0, top)
    return jnp.take_along_axis(listing, (jnp.arange(top)[None, :] + offset_by) % top, axis=1)


def portions_of(number_of, total, limit, slope, full):
    weights = [(1 << 20) // math.isqrt(rank ** slope) + 1 for rank in range(1, number_of + 1)]
    largest = limit if full else min(limit, max(-(-total // number_of), total * weights[0] // sum(weights)))
    least = 1 if total - largest >= number_of - 1 else 0
    counts, rest = [largest] + [least] * (number_of - 1), total - largest - least * (number_of - 1)
    while rest > 0:
        free = [i for i in range(1, number_of) if counts[i] < largest] or [i for i in range(1, number_of) if counts[i] < limit]
        whole, left = sum([weights[i] for i in free]), rest
        for i in free:
            extra = min(limit - counts[i], max(1, left * weights[i] // whole), rest)
            counts[i] = counts[i] + extra
            rest = rest - extra
    return np.array(counts)


def gaussian(own_key, dims, width, reach, cuts=(), kind=jnp.bfloat16):
    result = jax.random.normal(own_key, dims, jnp.float32) * width
    if len(cuts) > 0:
        result = shard_levels(own_key, dims, cuts, -0.22, 0.18) * result
    return jnp.clip(result, min=-reach, max=reach).astype(kind)


def setup_inputs(seed: int = 0) -> dict:
    keys = jax.random.split(jax.random.key(seed), 17)
    projected = draw_projected(jax.random.fold_in(keys[16], 71), 0)
    residual = draw_residual(jax.random.fold_in(keys[16], 71), 0)
    query_gain = draw_query_gain(jax.random.fold_in(keys[16], 71), 0)
    key_gain = draw_key_gain(jax.random.fold_in(keys[16], 71), 0)
    context_cache = gaussian(keys[4], (GROUPS, CONTEXT, 2, D), 1.0, 6.0, ((0, 64), (3, 4)))
    decode_cache = gaussian(keys[5], (DECODES, CACHE, 2, D), 1.0, 6.0, ((0, 64), (3, 4)))
    offsets = draw_offsets(jax.random.fold_in(keys[16], 71), 0)
    lengths = draw_lengths(jax.random.fold_in(keys[16], 71), 0)
    group_order = jax.random.permutation(keys[8], GROUPS).astype(jnp.int32)
    expert_ids_keys = jax.random.split(jax.random.fold_in(keys[9], 1), TOKENS // ROWS)
    expert_ids_turns = jax.random.permutation(jax.random.fold_in(keys[9], 3), TOKENS // ROWS)
    expert_ids = jax.vmap(lambda own, number: shared_out(jax.random.fold_in(keys[9], 2), own, number, ROWS, EXPERTS, TOPK, CAP, 2))(expert_ids_keys, expert_ids_turns).reshape((TOKENS, TOPK))
    out_weight = gaussian(keys[10], (D, D), D ** -0.5, 0.125, ((0, 4),))
    post_gain = jnp.clip(1.0 + 0.15 * jax.random.normal(keys[11], (D,), jnp.float32), 0.25, 1.75)
    router = draw_router(jax.random.fold_in(keys[16], 71), 0)
    gate_weight = gaussian(keys[13], (EXPERTS, D, EXP_FF), D ** -0.5, 0.125, ((0, 64), (2, 4)))
    up_weight = gaussian(keys[14], (EXPERTS, D, EXP_FF), D ** -0.5, 0.125, ((0, 64), (2, 4)))
    down_weight = gaussian(keys[15], (EXPERTS, EXP_FF, D), EXP_FF ** -0.5, 0.1875, ((0, 64), (1, 4)))
    return {"projected": projected, "residual": residual, "query_gain": query_gain, "key_gain": key_gain, "context_cache": context_cache, "decode_cache": decode_cache, "offsets": offsets, "lengths": lengths, "group_order": group_order, "expert_ids": expert_ids, "out_weight": out_weight, "post_gain": post_gain, "router": router, "gate_weight": gate_weight, "up_weight": up_weight, "down_weight": down_weight}


def rotate_rows(values, positions, head_size):
    row_count = values.shape[0]
    head_count = values.shape[1] // head_size
    half_size = head_size // 2
    shaped = values.reshape(row_count, head_count, head_size)
    frequency = 10000.0 ** (-2.0 * jnp.arange(half_size, dtype=jnp.float32) / head_size)
    angles = positions.astype(jnp.float32)[:, None] * frequency[None, :]
    cosine = jnp.cos(angles)[:, None, :]
    sine_part = jnp.sin(angles)[:, None, :]
    first_half = shaped[:, :, :half_size]
    second_half = shaped[:, :, half_size:]
    turned = jnp.concatenate([first_half * cosine - second_half * sine_part, second_half * cosine + first_half * sine_part], axis=2)
    return turned.reshape(row_count, head_count * head_size)

def attend(queries, key_rows, value_rows, usable):
    factor = 1.0 / math.sqrt(queries.shape[-1])
    scores = jnp.einsum('qhd,khd->hqk', queries.astype(jnp.float32), key_rows.astype(jnp.float32)) * factor
    scores = jnp.where(usable[None, :, :], scores, -jnp.inf)
    largest = lax.optimization_barrier(jnp.max(scores, axis=2, keepdims=True))
    weights = jnp.exp(scores - largest)
    shares = (weights / lax.optimization_barrier(jnp.sum(weights, axis=2, keepdims=True))).astype(jnp.bfloat16)
    mixture = jnp.einsum('hqk,khd->qhd', shares.astype(jnp.float32), value_rows.astype(jnp.float32))
    return mixture.astype(jnp.bfloat16)

def group_attention(query_rows, key_new, value_new, context, decode_cache, offset, decode_lengths, head_size, prefill_rows):
    width_here = query_rows.shape[1]
    head_count = width_here // head_size
    context_size = context.shape[0]

    def heads_view(matrix):
        return matrix.reshape(matrix.shape[:-1] + (head_count, head_size))
    prefill_keys = jnp.concatenate([context[:, 0], key_new[:prefill_rows]], axis=0)
    prefill_values = jnp.concatenate([context[:, 1], value_new[:prefill_rows]], axis=0)
    key_spot = jnp.arange(context_size + prefill_rows, dtype=jnp.int32)[None, :]
    query_spot = jnp.arange(prefill_rows, dtype=jnp.int32)[:, None]
    prefill_usable = jnp.where(key_spot < context_size, key_spot < offset, key_spot - context_size <= query_spot)
    prefill_out = attend(heads_view(query_rows[:prefill_rows]), heads_view(prefill_keys), heads_view(prefill_values), prefill_usable)
    decode_count = decode_cache.shape[0]
    cache_slots = decode_cache.shape[1]
    decode_keys = jnp.concatenate([decode_cache[:, :, 0], key_new[prefill_rows:, None, :]], axis=1)
    decode_values = jnp.concatenate([decode_cache[:, :, 1], value_new[prefill_rows:, None, :]], axis=1)
    slot_index = jnp.arange(cache_slots + 1, dtype=jnp.int32)[None, :]
    decode_usable = (slot_index < decode_lengths[:, None]) | (slot_index == cache_slots)
    decode_out = jax.vmap(attend)(heads_view(query_rows[prefill_rows:, None, :]), heads_view(decode_keys), heads_view(decode_values), decode_usable[:, None, :])
    return jnp.concatenate([prefill_out.reshape(prefill_rows, width_here), decode_out.reshape(decode_count, width_here)], axis=0)

def expert_apply(inputs, gate_matrix, up_matrix, down_matrix, pieces):
    gate_pre = jnp.dot(inputs, gate_matrix, preferred_element_type=jnp.float32)
    up_pre = jnp.dot(inputs, up_matrix, preferred_element_type=jnp.float32)
    hidden = (jax.nn.silu(gate_pre) * up_pre).astype(jnp.bfloat16)
    row_count = hidden.shape[0]
    per_piece = hidden.shape[1] // pieces
    pieces_out = jnp.einsum('rpf,pfd->rpd', hidden.reshape(row_count, pieces, per_piece).astype(jnp.float32), down_matrix.reshape(pieces, per_piece, -1).astype(jnp.float32))
    rounded = lax.optimization_barrier(pieces_out.astype(jnp.bfloat16))
    return lax.optimization_barrier(jnp.sum(rounded.astype(jnp.float32), axis=1)).astype(jnp.bfloat16)

def reference(projected, residual, query_gain, key_gain, context_cache, decode_cache, offsets, lengths, group_order, expert_ids, out_weight, post_gain, router, gate_weight, up_weight, down_weight):
    query_raw = projected[:, 0].astype(jnp.float32)
    key_raw = projected[:, 1].astype(jnp.float32)
    query_norm = query_raw * lax.rsqrt(lax.optimization_barrier(jnp.mean(query_raw * query_raw, axis=1, keepdims=True)) + 1e-05) * query_gain
    key_norm = key_raw * lax.rsqrt(lax.optimization_barrier(jnp.mean(key_raw * key_raw, axis=1, keepdims=True)) + 1e-05) * key_gain
    token_index = jnp.arange(TOKENS, dtype=jnp.int32)
    group_index = token_index // ROWS
    in_group = token_index % ROWS
    decode_index = jnp.clip(group_index * DEC_DEV + in_group - PRE_TOK, 0, DECODES - 1)
    positions = jnp.where(in_group < PRE_TOK, offsets[group_index] + in_group, lengths[decode_index])
    query_rot = rotate_rows(query_norm, positions, HEAD_DIM).astype(jnp.bfloat16)
    key_rot = rotate_rows(key_norm, positions, HEAD_DIM).astype(jnp.bfloat16)
    value_all = projected[:, 2]

    def one_group(group_id):
        first_row = (group_id * ROWS).astype(jnp.int32)
        query_rows = lax.dynamic_slice_in_dim(query_rot, first_row, ROWS, 0)
        key_rows = lax.dynamic_slice_in_dim(key_rot, first_row, ROWS, 0)
        value_rows = lax.dynamic_slice_in_dim(value_all, first_row, ROWS, 0)
        first_decode = (group_id * DEC_DEV).astype(jnp.int32)
        cache_rows = lax.dynamic_slice_in_dim(decode_cache, first_decode, DEC_DEV, 0)
        length_rows = lax.dynamic_slice_in_dim(lengths, first_decode, DEC_DEV, 0)
        return group_attention(query_rows, key_rows, value_rows, context_cache[group_id], cache_rows, offsets[group_id], length_rows, HEAD_DIM, PRE_TOK)
    attention = lax.map(one_group, jnp.arange(GROUPS, dtype=jnp.int32)).reshape(TOKENS, D)
    projected_out = jnp.dot(attention, out_weight, preferred_element_type=jnp.float32)
    hidden_state = (residual.astype(jnp.float32) + projected_out).astype(jnp.bfloat16)
    state_wide = hidden_state.astype(jnp.float32)
    normed = (state_wide * lax.rsqrt(lax.optimization_barrier(jnp.mean(state_wide * state_wide, axis=1, keepdims=True)) + 1e-05) * post_gain).astype(jnp.bfloat16)
    logits = jnp.dot(normed, router, preferred_element_type=jnp.float32)
    picked = jnp.take_along_axis(logits, expert_ids, axis=1)
    largest = lax.optimization_barrier(jnp.max(picked, axis=1, keepdims=True))
    raised = jnp.exp(picked - largest)
    gates = raised / lax.optimization_barrier(jnp.sum(raised, axis=1, keepdims=True))
    pair_token = jnp.arange(TOKENS * TOPK, dtype=jnp.int32) // TOPK
    pair_expert = expert_ids.reshape(TOKENS * TOPK)
    gate_flat = gates.reshape(TOKENS * TOPK)
    limit_rows = GROUPS * CAP

    def one_expert(running, expert):
        hits = pair_expert == expert
        chosen = jnp.nonzero(hits, size=limit_rows, fill_value=0)[0].astype(jnp.int32)
        matched = jnp.sum(hits.astype(jnp.int32))
        usable = jnp.arange(limit_rows, dtype=jnp.int32) < matched
        owners = pair_token[chosen]
        produced = expert_apply(normed[owners], gate_weight[expert], up_weight[expert], down_weight[expert], N_TP)
        weighting = jnp.where(usable, gate_flat[chosen], 0.0)
        return (running.at[owners].add(produced.astype(jnp.float32) * weighting[:, None]), None)
    expert_total, _ = lax.scan(one_expert, jnp.zeros((TOKENS, D), jnp.float32), jnp.arange(EXPERTS, dtype=jnp.int32))
    combined = (state_wide + expert_total).astype(jnp.bfloat16)
    ordered = jnp.zeros((GROUPS, ROWS, D), jnp.bfloat16).at[group_order].set(combined.reshape(GROUPS, ROWS, D))
    return ordered.reshape(TOKENS, D)
```

```python
import functools
import math

import jax
import jax.numpy as jnp
from jax import lax
from jax.experimental import pallas as pl
from jax.experimental.pallas import tpu as pltpu
from jax.sharding import Mesh, PartitionSpec as P

HEAD_DIM = 128
HEADS_HERE = 4
PRE = 128
DEC = 4
ROWS = PRE + DEC
SLOTS = 512
COLS = 512
FULL = 2048
EXPERTS = 64
CAP = 32
PLANES = 8
TP = 4
QUARTER = 8
PAIR_LANES = 512
VMEM_LIMIT = 56 * 1024 * 1024
NEAR = (0, -1, 1, -2, 2, -3, 3, 4)
BF = jnp.bfloat16
F32 = jnp.float32
VM = pl.BlockSpec(memory_space=pltpu.VMEM)
SM = pl.BlockSpec(memory_space=pltpu.SMEM)
HB = pl.BlockSpec(memory_space=pl.ANY)


def dot(a, b, contract_a=1, contract_b=0):
    return lax.dot_general(
        a, b, (((contract_a,), (contract_b,)), ((), ())), preferred_element_type=F32
    )


def iota(shape, axis):
    return lax.broadcasted_iota(jnp.int32, shape, axis)


def attention_kernel(
    numbers, proj, inv, cosine, sine, q_gain, k_gain, context, cache, weight, own, *rest
):
    sends, total = rest[:3], rest[3]
    head = pl.program_id(0)
    factor = 1.0 / math.sqrt(HEAD_DIM)
    cos_v, sin_v = cosine[...], sine[...]

    def rotated(part, gain, column):
        norm = proj[part].astype(F32) * inv[:, column : column + 1] * gain[...]
        return (norm * cos_v + pltpu.roll(norm, HEAD_DIM // 2, 1) * sin_v).astype(BF)

    qr = rotated(0, q_gain, 0)
    kr = rotated(1, k_gain, 1)
    value = proj[2]
    low = jnp.finfo(F32).min

    q_pre, k_pre, v_pre = qr[:PRE], kr[:PRE], value[:PRE]
    rows = context.reshape(2 * SLOTS, HEAD_DIM)[...]
    column = iota((PRE, 2 * SLOTS), 1)
    seen = ((column & 1) == 0) & (column < 2 * numbers[0])
    s_old = jnp.where(seen, dot(q_pre, rows, 1, 1) * factor, low)
    causal = iota((PRE, PRE), 1) <= iota((PRE, PRE), 0)
    s_new = jnp.where(causal, dot(q_pre, k_pre, 1, 1) * factor, low)
    top = jnp.maximum(
        jnp.max(s_old, axis=1, keepdims=True), jnp.max(s_new, axis=1, keepdims=True)
    )
    e_old = jnp.where(seen, jnp.exp(s_old - top), 0.0)
    e_new = jnp.where(causal, jnp.exp(s_new - top), 0.0)
    share = 1.0 / (
        jnp.sum(e_old, axis=1, keepdims=True) + jnp.sum(e_new, axis=1, keepdims=True)
    )
    p_old = pltpu.roll(e_old * share, 1, 1).astype(BF)
    p_new = (e_new * share).astype(BF)
    mixed_pre = (dot(p_old, rows) + dot(p_new, v_pre)).astype(BF)

    q_dec, k_dec, v_dec = qr[PRE:], kr[PRE:], value[PRE:]
    keys = cache.reshape(DEC * 2 * SLOTS, HEAD_DIM)[...]
    row = iota((DEC, DEC * 2 * SLOTS), 0)
    column = iota((DEC, DEC * 2 * SLOTS), 1)
    length = jnp.where(
        row == 0,
        numbers[1],
        jnp.where(row == 1, numbers[2], jnp.where(row == 2, numbers[3], numbers[4])),
    )
    place = column - row * (2 * SLOTS)
    seen = ((column & 1) == 0) & (place >= 0) & (place < 2 * length)
    s_old = jnp.where(seen, dot(q_dec, keys, 1, 1) * factor, low)
    s_own = (
        jnp.sum(q_dec.astype(F32) * k_dec.astype(F32), axis=1, keepdims=True) * factor
    )
    top = jnp.maximum(jnp.max(s_old, axis=1, keepdims=True), s_own)
    e_old = jnp.where(seen, jnp.exp(s_old - top), 0.0)
    e_own = jnp.exp(s_own - top)
    share = 1.0 / (jnp.sum(e_old, axis=1, keepdims=True) + e_own)
    p_old = pltpu.roll(e_old * share, 1, 1).astype(BF)
    p_own = (e_own * share).astype(BF).astype(F32)
    mixed_dec = (dot(p_old, keys) + p_own * v_dec.astype(F32)).astype(BF)

    w = weight[...]
    out_pre = dot(mixed_pre, w)
    out_dec = dot(mixed_dec, w)

    @pl.when(head == 0)
    def _():
        for block in range(TP):
            span = slice(block * COLS, (block + 1) * COLS)
            total[block, :PRE] = out_pre[:, span]
            total[block, PRE:] = out_dec[:, span]

    @pl.when(head > 0)
    def _():
        for block in range(TP):
            span = slice(block * COLS, (block + 1) * COLS)
            total[block, :PRE] += out_pre[:, span]
            total[block, PRE:] += out_dec[:, span]

    @pl.when(head == HEADS_HERE - 1)
    def _():
        own[...] = total[numbers[5]]
        for step in range(1, TP):
            sends[step - 1][...] = total[(numbers[5] + step) % TP].astype(BF)


def attention(numbers, proj, inv, cosine, sine, q_gain, k_gain, context, cache, weight):
    whole = lambda *shape: pl.BlockSpec(shape, lambda h: (0,) * len(shape))
    return pl.pallas_call(
        attention_kernel,
        grid=(HEADS_HERE,),
        in_specs=[
            SM,
            pl.BlockSpec((3, ROWS, HEAD_DIM), lambda h: (0, 0, h)),
            whole(ROWS, 2),
            whole(ROWS, HEAD_DIM),
            whole(ROWS, HEAD_DIM),
            pl.BlockSpec((1, HEAD_DIM), lambda h: (0, h)),
            pl.BlockSpec((1, HEAD_DIM), lambda h: (0, h)),
            pl.BlockSpec((1, SLOTS, 2, HEAD_DIM), lambda h: (0, 0, 0, h)),
            pl.BlockSpec((DEC, SLOTS, 2, HEAD_DIM), lambda h: (0, 0, 0, h)),
            pl.BlockSpec((HEAD_DIM, FULL), lambda h: (h, 0)),
        ],
        out_specs=[whole(ROWS, COLS)] * TP,
        out_shape=[jax.ShapeDtypeStruct((ROWS, COLS), F32)]
        + [jax.ShapeDtypeStruct((ROWS, COLS), BF)] * (TP - 1),
        scratch_shapes=[pltpu.VMEM((TP, ROWS, COLS), F32)],
        compiler_params=pltpu.CompilerParams(vmem_limit_bytes=VMEM_LIMIT),
        cost_estimate=pl.CostEstimate(
            flops=2_000_000_000, bytes_accessed=10_000_000, transcendentals=1_000_000
        ),
        name="attention",
    )(numbers, proj, inv, cosine, sine, q_gain, k_gain, context, cache, weight)


def slot_part(code):
    wide = code.astype(F32)
    return jnp.where(wide > 64.0, wide - 64.0, wide)


def pair_onehot(code, plane, second):
    place = iota((EXPERTS, PAIR_LANES), 1)
    device = place >> 4
    x, c, y = device & 3, (device >> 2) & 1, device >> 3
    expert = plane * PLANES + y * 2 + (x >> 1)
    spread = (iota((EXPERTS, PAIR_LANES), 0) == expert).astype(F32).astype(BF)
    slot = dot(slot_part(code).astype(BF), spread)
    place = iota((1, PAIR_LANES), 1)
    device = place >> 4
    quarter = (device & 1) * 2 + ((device >> 2) & 1)
    wanted = quarter * QUARTER + (place & 7) + 1
    wanted = jnp.where(((place >> 3) & 1) == second, wanted, -1).astype(F32)
    return (slot == wanted).astype(F32).astype(BF)


def expand_kernel(numbers, code, *refs):
    held, out = refs[:-1], refs[-1]
    plane = numbers[0]
    for pair in range(PLANES // 2):
        filled = None
        for second in range(2):
            position = 2 * pair + second
            hits = pair_onehot(
                code[(plane + NEAR[position] + PLANES) % PLANES], plane, second
            )
            if position < PLANES - 1:
                rows = held[position][...]
            else:
                rows = jnp.concatenate(
                    [held[PLANES - 1][...], held[PLANES][...]], axis=0
                )
            part = dot(hits, rows, 0, 0)
            filled = part if filled is None else filled + part
        out[:, 16 * pair : 16 * pair + 16, :] = filled.astype(BF).reshape(32, 16, COLS)


def expand(numbers, code, held):
    return pl.pallas_call(
        expand_kernel,
        in_specs=[SM, VM] + [VM] * len(held),
        out_specs=VM,
        out_shape=jax.ShapeDtypeStruct((32, 64, COLS), BF),
        compiler_params=pltpu.CompilerParams(vmem_limit_bytes=VMEM_LIMIT),
        cost_estimate=pl.CostEstimate(
            flops=700_000_000, bytes_accessed=4_000_000, transcendentals=0
        ),
        name="expand",
    )(numbers, code, *held)


def combine_kernel(numbers, order, code, answers, out):
    plane = numbers[0]
    pair = pl.program_id(0)
    rows = answers[...].reshape(PAIR_LANES, COLS)
    for second in range(2):
        group = order[2 * pair + second]
        hits = pair_onehot(code[group], plane, second)
        out[second] = dot(hits, rows).astype(BF)


def combine(numbers, order, code, answers):
    return pl.pallas_call(
        combine_kernel,
        grid=(PLANES // 2,),
        in_specs=[
            SM,
            SM,
            pl.BlockSpec((EXPERTS, ROWS, EXPERTS), lambda p: (0, 0, 0)),
            pl.BlockSpec((32, 16, COLS), lambda p: (0, p, 0)),
        ],
        out_specs=pl.BlockSpec((2, ROWS, COLS), lambda p: (p, 0, 0)),
        out_shape=jax.ShapeDtypeStruct((PLANES, ROWS, COLS), BF),
        compiler_params=pltpu.CompilerParams(vmem_limit_bytes=VMEM_LIMIT),
        cost_estimate=pl.CostEstimate(
            flops=700_000_000, bytes_accessed=4_000_000, transcendentals=0
        ),
        name="combine",
    )(numbers, order, code, answers)


def chosen_kernel(numbers, code, out):
    plane, expert, quarter = numbers[0], numbers[1], numbers[2]
    is_expert = iota((ROWS, EXPERTS), 1) == expert
    place = iota((1, 64), 1)
    wanted = quarter * QUARTER + (place & 7) + 1

    def one(column, carry):
        filled = jnp.zeros((64, EXPERTS), F32)
        for position in range(PLANES):
            z = (plane + NEAR[position] + PLANES) % PLANES
            rows = code[column * PLANES + z]
            slot = jnp.sum(
                jnp.where(is_expert, slot_part(rows), 0.0), axis=1, keepdims=True
            )
            aim = jnp.where((place >> 3) == position, wanted, -1).astype(F32)
            hits = (slot == aim).astype(F32).astype(BF)
            filled = filled + dot(hits, rows, 0, 0)
        out[column] = filled
        return carry

    lax.fori_loop(0, PLANES, one, 0)


def chosen_rows(numbers, code):
    return pl.pallas_call(
        chosen_kernel,
        in_specs=[SM, VM],
        out_specs=VM,
        out_shape=jax.ShapeDtypeStruct((PLANES, 64, EXPERTS), F32),
        compiler_params=pltpu.CompilerParams(vmem_limit_bytes=VMEM_LIMIT),
        cost_estimate=pl.CostEstimate(
            flops=200_000_000, bytes_accessed=2_000_000, transcendentals=0
        ),
        name="chosen_rows",
    )(numbers, code)


def expert_kernel(numbers, arrived, codes, origin, gain, router, *refs):
    parts, out = refs[:18], refs[18]
    weights, sems = refs[19:22], refs[22]
    at_home = numbers[3]
    for kind in range(3):
        own, first, other_own, second, other_first, other_second = parts[
            6 * kind : 6 * kind + 6
        ]

        @pl.when(at_home == 1)
        def _():
            pltpu.make_async_copy(own, weights[kind].at[0], sems.at[kind, 0]).start()
            pltpu.make_async_copy(
                other_second, weights[kind].at[3], sems.at[kind, 3]
            ).start()

        @pl.when(at_home == 0)
        def _():
            pltpu.make_async_copy(
                other_own, weights[kind].at[0], sems.at[kind, 0]
            ).start()
            pltpu.make_async_copy(second, weights[kind].at[3], sems.at[kind, 3]).start()

        pltpu.make_async_copy(first, weights[kind].at[1], sems.at[kind, 1]).start()
        pltpu.make_async_copy(
            other_first, weights[kind].at[2], sems.at[kind, 2]
        ).start()

    wide = []
    squares = jnp.zeros((512, 1), F32)
    for x in range(TP):
        part = arrived[:, x].reshape(512, COLS).astype(F32)
        squares = squares + jnp.sum(part * part, axis=1, keepdims=True)
    scale = lax.rsqrt(squares / FULL + 1e-05)
    logits = jnp.zeros((512, EXPERTS), F32)
    for x in range(TP):
        span = slice(x * COLS, (x + 1) * COLS)
        part = arrived[:, x].reshape(512, COLS).astype(F32)
        normed = (part * scale * gain[:, span]).astype(BF)
        wide.append(normed)
        logits = logits + dot(normed, router[:, span], 1, 1)
    code = codes[...].reshape(512, EXPERTS)
    chosen = code > 0.0
    is_expert = iota((512, EXPERTS), 1) == numbers[1]
    top = jnp.max(jnp.where(chosen, logits, jnp.finfo(F32).min), axis=1, keepdims=True)
    raised = jnp.where(chosen, jnp.exp(jnp.minimum(logits - top, 0.0)), 0.0)
    bottom = jnp.sum(raised, axis=1, keepdims=True)
    share = jnp.sum(jnp.where(is_expert, raised, 0.0), axis=1, keepdims=True)
    gate = jnp.where(bottom > 0.0, share / jnp.where(bottom > 0.0, bottom, 1.0), 0.0)
    mark = jnp.sum(jnp.where(is_expert, code, 0.0), axis=1, keepdims=True)
    first_choice = (mark > 64.0).astype(F32)

    total = None
    for quarter in range(4):
        for kind in range(3):
            source = parts[6 * kind + 1]
            pltpu.make_async_copy(
                source, weights[kind].at[quarter], sems.at[kind, quarter]
            ).wait()
        gate_pre = jnp.zeros((512, 256), F32)
        up_pre = jnp.zeros((512, 256), F32)
        for x in range(TP):
            span = slice(x * COLS, (x + 1) * COLS)
            gate_pre = gate_pre + dot(wide[x], weights[0][quarter, span, :])
            up_pre = up_pre + dot(wide[x], weights[1][quarter, span, :])
        hidden = (gate_pre / (1.0 + jnp.exp(-gate_pre)) * up_pre).astype(BF)
        term = dot(hidden, weights[2][quarter])
        total = term if total is None else total + term
    result = total.astype(BF).astype(F32) * gate
    move = (origin[...] == iota((512, 512), 1)).astype(F32).astype(BF)
    for x in range(TP):
        span = slice(x * COLS, (x + 1) * COLS)
        part = arrived[:, x].reshape(512, COLS).astype(F32)
        piece = (result[:, span] + first_choice * part).astype(BF)
        out[:, x] = dot(move, piece).astype(BF).reshape(PLANES, 64, COLS)


def expert(numbers, arrived, codes, origin, gain, router, parts):
    return pl.pallas_call(
        expert_kernel,
        in_specs=[SM] + [VM] * 5 + [HB] * 18,
        out_specs=VM,
        out_shape=jax.ShapeDtypeStruct((PLANES, TP, 64, COLS), BF),
        scratch_shapes=[
            pltpu.VMEM((4, FULL, 256), BF),
            pltpu.VMEM((4, FULL, 256), BF),
            pltpu.VMEM((4, 256, FULL), BF),
            pltpu.SemaphoreType.DMA((3, 4)),
        ],
        compiler_params=pltpu.CompilerParams(vmem_limit_bytes=VMEM_LIMIT),
        cost_estimate=pl.CostEstimate(
            flops=6_500_000_000, bytes_accessed=20_000_000, transcendentals=500_000
        ),
        name="expert",
    )(numbers, arrived, codes, origin, gain, router, *parts)


def pair_moves():
    at = lambda core, x: core * TP + x
    over = lambda d: (d + TP) % (2 * TP)
    first = [
        (at(0, 0), at(0, 1)),
        (at(0, 1), at(0, 0)),
        (at(0, 2), at(1, 1)),
        (at(0, 3), at(1, 0)),
        (at(1, 2), at(1, 3)),
        (at(1, 3), at(1, 2)),
        (at(1, 1), at(0, 2)),
        (at(1, 0), at(0, 3)),
    ]
    second = [
        (at(1, 0), at(1, 1)),
        (at(1, 1), at(1, 0)),
        (at(0, 2), at(0, 3)),
        (at(0, 3), at(0, 2)),
    ]
    home = [at(0, 0), at(0, 1), at(1, 2), at(1, 3)]
    return (
        first,
        second,
        [(d, over(d)) for d in home],
        [(d, over(d)) for d in range(2 * TP)],
        [(over(d), d) for d in home],
    )


def gathered_weight(own):
    first_move, second_move, out_of_home, both, to_home = pair_moves()
    axes = ("c", "tp")
    first = lax.ppermute(own, axes, first_move)
    other_own = lax.ppermute(own, axes, out_of_home)
    second = lax.ppermute(first, axes, second_move)
    other_first = lax.ppermute(first, axes, both)
    other_second = lax.ppermute(second, axes, to_home)
    return [own, first, other_own, second, other_first, other_second]


def around(value, axis, step):
    count = lax.axis_size(axis)
    return lax.ppermute(value, axis, [(i, (i + step) % count) for i in range(count)])


def gather_column(value):
    up = [value]
    down = [value]
    for _ in range(3):
        up.append(around(up[-1], "z", 1))
        down.append(around(down[-1], "z", -1))
    return [
        value,
        up[1],
        down[1],
        up[2],
        down[2],
        up[3],
        down[3],
        around(up[3][:64], "z", 1),
        around(down[3][64:], "z", -1),
    ]


def per_device(
    projected,
    residual,
    query_gain,
    key_gain,
    context_cache,
    decode_cache,
    offsets,
    lengths,
    group_order,
    expert_ids,
    out_weight,
    post_gain,
    router,
    gate_weight,
    up_weight,
    down_weight,
):
    z, y, c, tp = (lax.axis_index(name) for name in ("z", "y", "c", "tp"))
    column = y * 2 + c

    every = jnp.arange(EXPERTS, dtype=jnp.int32)
    chosen = jnp.zeros((ROWS, EXPERTS), jnp.bool_)
    for k in range(expert_ids.shape[1]):
        chosen = chosen | (expert_ids[:, k : k + 1] == every[None, :])
    below = jnp.arange(ROWS)[:, None] >= jnp.arange(ROWS)[None, :]
    slot = dot(below.astype(BF), chosen.astype(BF))
    first_choice = expert_ids[:, :1] == every[None, :]
    code = jnp.where(chosen, slot + 64.0 * first_choice, 0.0).astype(BF)
    code_column = lax.all_gather(code, "z", axis=0)
    code_all = lax.all_gather(code_column, ("y", "c"), axis=0).reshape(
        EXPERTS, ROWS, EXPERTS
    )

    parts = (
        gathered_weight(gate_weight[0])
        + gathered_weight(up_weight[0])
        + gathered_weight(down_weight[0])
    )

    proj = jnp.transpose(projected, (1, 0, 2))
    raw = proj[:2].astype(F32)
    squares = lax.psum(jnp.sum(raw * raw, axis=2), "tp")
    inv = lax.rsqrt(squares / FULL + 1e-05).T
    spot = jnp.arange(ROWS, dtype=jnp.int32)
    positions = offsets[0] + spot
    for i in range(DEC):
        positions = jnp.where(spot == PRE + i, lengths[i], positions)
    half = HEAD_DIM // 2
    frequency = 10000.0 ** (-2.0 * jnp.arange(half, dtype=F32) / HEAD_DIM)
    angles = positions.astype(F32)[:, None] * frequency[None, :]
    cosine, sine = jnp.cos(angles), jnp.sin(angles)
    cosine = jnp.concatenate([cosine, cosine], axis=1)
    sine = jnp.concatenate([-sine, sine], axis=1)
    numbers = jnp.concatenate([offsets, lengths, tp[None].astype(jnp.int32)])
    own, *sends = attention(
        numbers,
        proj,
        inv,
        cosine,
        sine,
        query_gain[None],
        key_gain[None],
        context_cache,
        decode_cache,
        out_weight,
    )
    state = own
    for step in range(1, TP):
        state = state + around(sends[step - 1], "tp", step).astype(F32)
    residual_here = lax.dynamic_slice_in_dim(residual, tp * COLS, COLS, 1)
    state = (residual_here.astype(F32) + state).astype(BF)

    serves = y * 2 + tp // 2
    quarter = (tp % 2) * 2 + c
    at_home = (tp // 2 == c).astype(jnp.int32)
    numbers = jnp.stack([z, z * PLANES + serves, quarter, at_home]).astype(jnp.int32)
    codes = chosen_rows(numbers, code_all)
    outgoing = expand(numbers, code_column, gather_column(state))
    plane = ("y", "c", "tp")
    arrived = lax.all_to_all(outgoing, plane, split_axis=0, concat_axis=0, tiled=True)

    groups = jnp.arange(EXPERTS, dtype=jnp.int32)
    inverse = jnp.sum(
        jnp.where(group_order[None, :] == groups[:, None], groups[None, :], 0), axis=1
    )
    source = inverse.reshape(PLANES, PLANES).T
    source_z, source_column = source // PLANES, source % PLANES
    distance = (source_z - z + PLANES) % PLANES
    position = jnp.zeros_like(distance)
    for spot_here, near in enumerate(NEAR):
        position = jnp.where(distance == near % PLANES, spot_here, position)
    origin = (source_column * PLANES + position)[:, :, None] * QUARTER + jnp.arange(
        QUARTER, dtype=jnp.int32
    )
    result = expert(
        numbers,
        arrived.reshape(PLANES, TP, 64, COLS),
        codes,
        origin.reshape(512, 1),
        post_gain[None],
        router.T,
        parts,
    )
    answers = lax.all_to_all(
        result.reshape(32, 64, COLS), plane, split_axis=0, concat_axis=0, tiled=True
    )
    mine = lax.dynamic_index_in_dim(source, column, 0, keepdims=False)
    rows_in_code = (mine % PLANES) * PLANES + mine // PLANES
    sums = combine(numbers, rows_in_code, code_all, answers)
    return lax.psum_scatter(sums, "z", scatter_dimension=0)


def solution(mesh):
    split = Mesh(mesh.devices.reshape(PLANES, 4, 2, TP), ("z", "y", "c", "tp"))
    req = ("z", "y", "c")
    return jax.shard_map(
        per_device,
        mesh=split,
        in_specs=(
            P(req, None, "tp"),
            P(req, None),
            P("tp"),
            P("tp"),
            P(req, None, None, "tp"),
            P(req, None, None, "tp"),
            P(req),
            P(req),
            P(),
            P(req, None),
            P("tp", None),
            P(),
            P(),
            P(req, None, "tp"),
            P(req, None, "tp"),
            P(req, "tp", None),
        ),
        out_specs=P(req, "tp"),
        check_vma=False,
    )
```

```python
import functools
import math

import jax
import jax.numpy as jnp
from jax import lax
from jax.experimental import pallas as pl
from jax.experimental.pallas import tpu as pltpu
from jax.sharding import Mesh, PartitionSpec as P

HEAD_DIM = 128
HEADS_HERE = 4
PRE = 128
DEC = 4
ROWS = PRE + DEC
SLOTS = 512
COLS = 512
FULL = 2048
EXPERTS = 64
LANES = 128
CAP = 32
PLANES = 8
TP = 4
QUARTER = 8
PAIR_LANES = 512
VMEM_LIMIT = 56 * 1024 * 1024
NEAR = (0, -1, 1, -2, 2, -3, 3, 4)
BF = jnp.bfloat16
F32 = jnp.float32
VM = pl.BlockSpec(memory_space=pltpu.VMEM)
SM = pl.BlockSpec(memory_space=pltpu.SMEM)
HB = pl.BlockSpec(memory_space=pl.ANY)


def dot(a, b, contract_a=1, contract_b=0):
    return lax.dot_general(
        a, b, (((contract_a,), (contract_b,)), ((), ())), preferred_element_type=F32
    )


def iota(shape, axis):
    return lax.broadcasted_iota(jnp.int32, shape, axis)


def attention_kernel(
    numbers, proj, inv, cosine, sine, q_gain, k_gain, context, cache, weight, own, *rest
):
    sends, total = rest[:3], rest[3]
    head = pl.program_id(0)
    factor = 1.0 / math.sqrt(HEAD_DIM)
    cos_v, sin_v = cosine[...], sine[...]

    def rotated(part, gain, column):
        norm = proj[part].astype(F32) * inv[:, column : column + 1] * gain[...]
        return (norm * cos_v + pltpu.roll(norm, HEAD_DIM // 2, 1) * sin_v).astype(BF)

    qr = rotated(0, q_gain, 0)
    kr = rotated(1, k_gain, 1)
    value = proj[2]
    low = jnp.finfo(F32).min

    q_pre, k_pre, v_pre = qr[:PRE], kr[:PRE], value[:PRE]
    rows = context.reshape(2 * SLOTS, HEAD_DIM)[...]
    column = iota((PRE, 2 * SLOTS), 1)
    seen = ((column & 1) == 0) & (column < 2 * numbers[0])
    s_old = jnp.where(seen, dot(q_pre, rows, 1, 1) * factor, low)
    causal = iota((PRE, PRE), 1) <= iota((PRE, PRE), 0)
    s_new = jnp.where(causal, dot(q_pre, k_pre, 1, 1) * factor, low)
    top = jnp.maximum(
        jnp.max(s_old, axis=1, keepdims=True), jnp.max(s_new, axis=1, keepdims=True)
    )
    e_old = jnp.where(seen, jnp.exp(s_old - top), 0.0)
    e_new = jnp.where(causal, jnp.exp(s_new - top), 0.0)
    share = 1.0 / (
        jnp.sum(e_old, axis=1, keepdims=True) + jnp.sum(e_new, axis=1, keepdims=True)
    )
    p_old = pltpu.roll(e_old * share, 1, 1).astype(BF)
    p_new = (e_new * share).astype(BF)
    mixed_pre = (dot(p_old, rows) + dot(p_new, v_pre)).astype(BF)

    q_dec, k_dec, v_dec = qr[PRE:], kr[PRE:], value[PRE:]
    keys = cache.reshape(DEC * 2 * SLOTS, HEAD_DIM)[...]
    row = iota((DEC, DEC * 2 * SLOTS), 0)
    column = iota((DEC, DEC * 2 * SLOTS), 1)
    length = jnp.where(
        row == 0,
        numbers[1],
        jnp.where(row == 1, numbers[2], jnp.where(row == 2, numbers[3], numbers[4])),
    )
    place = column - row * (2 * SLOTS)
    seen = ((column & 1) == 0) & (place >= 0) & (place < 2 * length)
    s_old = jnp.where(seen, dot(q_dec, keys, 1, 1) * factor, low)
    s_own = (
        jnp.sum(q_dec.astype(F32) * k_dec.astype(F32), axis=1, keepdims=True) * factor
    )
    top = jnp.maximum(jnp.max(s_old, axis=1, keepdims=True), s_own)
    e_old = jnp.where(seen, jnp.exp(s_old - top), 0.0)
    e_own = jnp.exp(s_own - top)
    share = 1.0 / (jnp.sum(e_old, axis=1, keepdims=True) + e_own)
    p_old = pltpu.roll(e_old * share, 1, 1).astype(BF)
    p_own = (e_own * share).astype(BF).astype(F32)
    mixed_dec = (dot(p_old, keys) + p_own * v_dec.astype(F32)).astype(BF)

    w = weight[...]
    out_pre = dot(mixed_pre, w)
    out_dec = dot(mixed_dec, w)

    @pl.when(head == 0)
    def _():
        for block in range(TP):
            span = slice(block * COLS, (block + 1) * COLS)
            total[block, :PRE] = out_pre[:, span]
            total[block, PRE:] = out_dec[:, span]

    @pl.when(head > 0)
    def _():
        for block in range(TP):
            span = slice(block * COLS, (block + 1) * COLS)
            total[block, :PRE] += out_pre[:, span]
            total[block, PRE:] += out_dec[:, span]

    @pl.when(head == HEADS_HERE - 1)
    def _():
        own[...] = total[numbers[5]]
        for step in range(1, TP):
            sends[step - 1][...] = total[(numbers[5] + step) % TP].astype(BF)


def attention(numbers, proj, inv, cosine, sine, q_gain, k_gain, context, cache, weight):
    whole = lambda *shape: pl.BlockSpec(shape, lambda h: (0,) * len(shape))
    return pl.pallas_call(
        attention_kernel,
        grid=(HEADS_HERE,),
        in_specs=[
            SM,
            pl.BlockSpec((3, ROWS, HEAD_DIM), lambda h: (0, 0, h)),
            whole(ROWS, 2),
            whole(ROWS, HEAD_DIM),
            whole(ROWS, HEAD_DIM),
            pl.BlockSpec((1, HEAD_DIM), lambda h: (0, h)),
            pl.BlockSpec((1, HEAD_DIM), lambda h: (0, h)),
            pl.BlockSpec((1, SLOTS, 2, HEAD_DIM), lambda h: (0, 0, 0, h)),
            pl.BlockSpec((DEC, SLOTS, 2, HEAD_DIM), lambda h: (0, 0, 0, h)),
            pl.BlockSpec((HEAD_DIM, FULL), lambda h: (h, 0)),
        ],
        out_specs=[whole(ROWS, COLS)] * TP,
        out_shape=[jax.ShapeDtypeStruct((ROWS, COLS), F32)]
        + [jax.ShapeDtypeStruct((ROWS, COLS), BF)] * (TP - 1),
        scratch_shapes=[pltpu.VMEM((TP, ROWS, COLS), F32)],
        compiler_params=pltpu.CompilerParams(vmem_limit_bytes=VMEM_LIMIT),
        cost_estimate=pl.CostEstimate(
            flops=2_000_000_000, bytes_accessed=10_000_000, transcendentals=1_000_000
        ),
        name="attention",
    )(numbers, proj, inv, cosine, sine, q_gain, k_gain, context, cache, weight)


def slot_part(code):
    wide = code.astype(F32)
    return jnp.where(wide > 64.0, wide - 64.0, wide)


def pair_onehot(code, plane, second):
    place = iota((LANES, PAIR_LANES), 1)
    device = place >> 4
    x, c, y = device & 3, (device >> 2) & 1, device >> 3
    expert = plane * PLANES + y * 2 + (x >> 1)
    spread = (iota((LANES, PAIR_LANES), 0) == expert).astype(F32).astype(BF)
    slot = dot(slot_part(code).astype(BF), spread)
    place = iota((1, PAIR_LANES), 1)
    device = place >> 4
    quarter = (device & 1) * 2 + ((device >> 2) & 1)
    wanted = quarter * QUARTER + (place & 7) + 1
    wanted = jnp.where(((place >> 3) & 1) == second, wanted, -1).astype(F32)
    return (slot == wanted).astype(F32).astype(BF)


def expand_kernel(numbers, code, *refs):
    held, out = refs[:-1], refs[-1]
    plane = numbers[0]
    for pair in range(PLANES // 2):
        filled = None
        for second in range(2):
            position = 2 * pair + second
            hits = pair_onehot(
                code[(plane + NEAR[position] + PLANES) % PLANES], plane, second
            )
            if position < PLANES - 1:
                rows = held[position][...]
            else:
                rows = jnp.concatenate(
                    [held[PLANES - 1][...], held[PLANES][...]], axis=0
                )
            part = dot(hits, rows, 0, 0)
            filled = part if filled is None else filled + part
        out[:, 16 * pair : 16 * pair + 16, :] = filled.astype(BF).reshape(32, 16, COLS)


def expand(numbers, code, held):
    return pl.pallas_call(
        expand_kernel,
        in_specs=[SM, VM] + [VM] * len(held),
        out_specs=VM,
        out_shape=jax.ShapeDtypeStruct((32, 64, COLS), BF),
        compiler_params=pltpu.CompilerParams(vmem_limit_bytes=VMEM_LIMIT),
        cost_estimate=pl.CostEstimate(
            flops=700_000_000, bytes_accessed=4_000_000, transcendentals=0
        ),
        name="expand",
    )(numbers, code, *held)


def combine_kernel(numbers, order, code, answers, out):
    plane = numbers[0]
    pair = pl.program_id(0)
    rows = answers[...].reshape(PAIR_LANES, COLS)
    for second in range(2):
        group = order[2 * pair + second]
        hits = pair_onehot(code[group], plane, second)
        out[second] = dot(hits, rows).astype(BF)


def combine(numbers, order, code, answers):
    return pl.pallas_call(
        combine_kernel,
        grid=(PLANES // 2,),
        in_specs=[
            SM,
            SM,
            pl.BlockSpec((EXPERTS, ROWS, LANES), lambda p: (0, 0, 0)),
            pl.BlockSpec((32, 16, COLS), lambda p: (0, p, 0)),
        ],
        out_specs=pl.BlockSpec((2, ROWS, COLS), lambda p: (p, 0, 0)),
        out_shape=jax.ShapeDtypeStruct((PLANES, ROWS, COLS), BF),
        compiler_params=pltpu.CompilerParams(vmem_limit_bytes=VMEM_LIMIT),
        cost_estimate=pl.CostEstimate(
            flops=700_000_000, bytes_accessed=4_000_000, transcendentals=0
        ),
        name="combine",
    )(numbers, order, code, answers)


def chosen_kernel(numbers, code, out):
    plane, expert, quarter = numbers[0], numbers[1], numbers[2]
    is_expert = iota((ROWS, LANES), 1) == expert
    place = iota((1, 64), 1)
    wanted = quarter * QUARTER + (place & 7) + 1

    def one(column, carry):
        filled = jnp.zeros((64, LANES), F32)
        for position in range(PLANES):
            z = (plane + NEAR[position] + PLANES) % PLANES
            rows = code[column * PLANES + z]
            slot = jnp.sum(
                jnp.where(is_expert, slot_part(rows), 0.0), axis=1, keepdims=True
            )
            aim = jnp.where((place >> 3) == position, wanted, -1).astype(F32)
            hits = (slot == aim).astype(F32).astype(BF)
            filled = filled + dot(hits, rows, 0, 0)
        out[column] = filled
        return carry

    lax.fori_loop(0, PLANES, one, 0)


def chosen_rows(numbers, code):
    return pl.pallas_call(
        chosen_kernel,
        in_specs=[SM, VM],
        out_specs=VM,
        out_shape=jax.ShapeDtypeStruct((PLANES, 64, LANES), F32),
        compiler_params=pltpu.CompilerParams(vmem_limit_bytes=VMEM_LIMIT),
        cost_estimate=pl.CostEstimate(
            flops=200_000_000, bytes_accessed=2_000_000, transcendentals=0
        ),
        name="chosen_rows",
    )(numbers, code)


def expert_kernel(numbers, arrived, codes, origin, gain, router, *refs):
    parts, out = refs[:18], refs[18]
    weights, normed, hidden, sems = refs[19:22], refs[22], refs[23], refs[24]
    at_home = numbers[3]

    def place(kind, quarter):
        if kind < 2:
            return weights[kind].at[quarter]
        return weights[2].at[quarter * 256 : (quarter + 1) * 256]

    def bring(source, kind, quarter):
        pltpu.make_async_copy(
            source, place(kind, quarter), sems.at[kind, quarter]
        ).start()

    def arrival(kind, quarter):
        return pltpu.make_async_copy(
            parts[6 * kind + 1], place(kind, quarter), sems.at[kind, quarter]
        )

    for kind in range(3):
        own, first, other_own, second, other_first, other_second = parts[
            6 * kind : 6 * kind + 6
        ]

        @pl.when(at_home == 1)
        def _():
            bring(own, kind, 0)
            bring(other_second, kind, 3)

        @pl.when(at_home == 0)
        def _():
            bring(other_own, kind, 0)
            bring(second, kind, 3)

        bring(first, kind, 1)
        bring(other_first, kind, 2)

    squares = jnp.zeros((512, 1), F32)
    for x in range(TP):
        part = arrived[:, x].reshape(512, COLS).astype(F32)
        squares = squares + jnp.sum(part * part, axis=1, keepdims=True)
    scale = lax.rsqrt(squares / FULL + 1e-05)
    for x in range(TP):
        span = slice(x * COLS, (x + 1) * COLS)
        part = arrived[:, x].reshape(512, COLS).astype(F32)
        normed[:, span] = (part * scale * gain[:, span]).astype(BF)
    logits = dot(normed[...], router[...], 1, 1)
    code = codes[...].reshape(512, LANES)[:, :EXPERTS]
    chosen = code > 0.0
    is_expert = iota((512, EXPERTS), 1) == numbers[1]
    top = jnp.max(jnp.where(chosen, logits, jnp.finfo(F32).min), axis=1, keepdims=True)
    raised = jnp.where(chosen, jnp.exp(jnp.minimum(logits - top, 0.0)), 0.0)
    bottom = jnp.sum(raised, axis=1, keepdims=True)
    share = jnp.sum(jnp.where(is_expert, raised, 0.0), axis=1, keepdims=True)
    gate = jnp.where(bottom > 0.0, share / jnp.where(bottom > 0.0, bottom, 1.0), 0.0)
    mark = jnp.sum(jnp.where(is_expert, code, 0.0), axis=1, keepdims=True)
    first_choice = (mark > 64.0).astype(F32)

    for quarter in range(4):
        for kind in range(2):
            arrival(kind, quarter).wait()
        gate_pre = dot(normed[...], weights[0][quarter])
        up_pre = dot(normed[...], weights[1][quarter])
        hidden[:, quarter * 256 : (quarter + 1) * 256] = (
            gate_pre / (1.0 + jnp.exp(-gate_pre)) * up_pre
        ).astype(BF)
    for quarter in range(4):
        arrival(2, quarter).wait()
    move = (origin[...] == iota((512, 512), 1)).astype(F32).astype(BF)
    for x in range(TP):
        span = slice(x * COLS, (x + 1) * COLS)
        part = arrived[:, x].reshape(512, COLS).astype(F32)
        result = dot(hidden[...], weights[2][:, span]).astype(BF).astype(F32) * gate
        piece = (result + first_choice * part).astype(BF)
        out[:, x] = dot(move, piece).astype(BF).reshape(PLANES, 64, COLS)


def expert(numbers, arrived, codes, origin, gain, router, parts):
    return pl.pallas_call(
        expert_kernel,
        in_specs=[SM] + [VM] * 5 + [HB] * 18,
        out_specs=VM,
        out_shape=jax.ShapeDtypeStruct((PLANES, TP, 64, COLS), BF),
        scratch_shapes=[
            pltpu.VMEM((4, FULL, 256), BF),
            pltpu.VMEM((4, FULL, 256), BF),
            pltpu.VMEM((1024, FULL), BF),
            pltpu.VMEM((512, FULL), BF),
            pltpu.VMEM((512, 1024), BF),
            pltpu.SemaphoreType.DMA((3, 4)),
        ],
        compiler_params=pltpu.CompilerParams(vmem_limit_bytes=VMEM_LIMIT),
        cost_estimate=pl.CostEstimate(
            flops=6_500_000_000, bytes_accessed=20_000_000, transcendentals=500_000
        ),
        name="expert",
    )(numbers, arrived, codes, origin, gain, router, *parts)


def pair_moves():
    at = lambda core, x: core * TP + x
    over = lambda d: (d + TP) % (2 * TP)
    first = [
        (at(0, 0), at(0, 1)),
        (at(0, 1), at(0, 0)),
        (at(0, 2), at(1, 1)),
        (at(0, 3), at(1, 0)),
        (at(1, 2), at(1, 3)),
        (at(1, 3), at(1, 2)),
        (at(1, 1), at(0, 2)),
        (at(1, 0), at(0, 3)),
    ]
    second = [
        (at(1, 0), at(1, 1)),
        (at(1, 1), at(1, 0)),
        (at(0, 2), at(0, 3)),
        (at(0, 3), at(0, 2)),
    ]
    home = [at(0, 0), at(0, 1), at(1, 2), at(1, 3)]
    return (
        first,
        second,
        [(d, over(d)) for d in home],
        [(d, over(d)) for d in range(2 * TP)],
        [(over(d), d) for d in home],
    )


PAIR = ("c", "tp")


def tied(*values):
    return lax.optimization_barrier(values)


def around(value, axis, step):
    count = lax.axis_size(axis)
    return lax.ppermute(value, axis, [(i, (i + step) % count) for i in range(count)])


def gather_column(value, code):
    up = [value]
    down = [value]
    for step in range(3):
        up.append(around(up[-1], "z", 1))
        down.append(around(down[-1], "z", -1))
        if step == 1:
            up[2], down[2], code = tied(up[2], down[2], code)
    return [
        value,
        up[1],
        down[1],
        up[2],
        down[2],
        up[3],
        down[3],
        around(up[3][:64], "z", 1),
        around(down[3][64:], "z", -1),
    ], code


def per_device(
    projected,
    residual,
    query_gain,
    key_gain,
    context_cache,
    decode_cache,
    offsets,
    lengths,
    group_order,
    expert_ids,
    out_weight,
    post_gain,
    router,
    gate_weight,
    up_weight,
    down_weight,
):
    z, y, c, tp = (lax.axis_index(name) for name in ("z", "y", "c", "tp"))
    column = y * 2 + c

    every = jnp.arange(LANES, dtype=jnp.int32)
    chosen = jnp.zeros((ROWS, LANES), jnp.bool_)
    for k in range(expert_ids.shape[1]):
        chosen = chosen | (expert_ids[:, k : k + 1] == every[None, :])
    below = jnp.arange(ROWS)[:, None] >= jnp.arange(ROWS)[None, :]
    slot = dot(below.astype(BF), chosen.astype(BF))
    first_choice = expert_ids[:, :1] == every[None, :]
    code = jnp.where(chosen, slot + 64.0 * first_choice, 0.0).astype(BF)
    widened = jnp.concatenate([code] + [jnp.zeros_like(code)] * 3, axis=1)
    code_column = lax.all_gather(widened, "z", axis=0)

    first_move, second_move, out_of_home, both, to_home = pair_moves()
    owns = [gate_weight[0], up_weight[0], down_weight[0]]
    firsts = [lax.ppermute(own, PAIR, first_move) for own in owns]

    proj = jnp.transpose(projected, (1, 0, 2))
    raw = proj[:2].astype(F32)
    squares = jnp.sum(raw * raw, axis=2)
    shared = [around(squares, "tp", step) for step in range(1, TP)]
    squares = squares + shared[0] + shared[1] + shared[2]
    squares, firsts[0] = tied(squares, firsts[0])
    inv = lax.rsqrt(squares / FULL + 1e-05).T
    spot = jnp.arange(ROWS, dtype=jnp.int32)
    positions = offsets[0] + spot
    for i in range(DEC):
        positions = jnp.where(spot == PRE + i, lengths[i], positions)
    half = HEAD_DIM // 2
    frequency = 10000.0 ** (-2.0 * jnp.arange(half, dtype=F32) / HEAD_DIM)
    angles = positions.astype(F32)[:, None] * frequency[None, :]
    cosine, sine = jnp.cos(angles), jnp.sin(angles)
    cosine = jnp.concatenate([cosine, cosine], axis=1)
    sine = jnp.concatenate([-sine, sine], axis=1)
    numbers = jnp.concatenate([offsets, lengths, tp[None].astype(jnp.int32)])
    own, *sends = attention(
        numbers,
        proj,
        inv,
        cosine,
        sine,
        query_gain[None],
        key_gain[None],
        context_cache,
        decode_cache,
        out_weight,
    )
    *sends, firsts[1], firsts[2] = tied(*sends, firsts[1], firsts[2])
    seconds = [lax.ppermute(first, PAIR, second_move) for first in firsts]
    state = own
    for step in range(1, TP):
        state = state + around(sends[step - 1], "tp", step).astype(F32)
    residual_here = lax.dynamic_slice_in_dim(residual, tp * COLS, COLS, 1)
    state = (residual_here.astype(F32) + state).astype(BF)
    column_states, code_column = gather_column(state, code_column)
    code_column = code_column[:, :, :LANES]
    code_all = lax.all_gather(code_column, ("y", "c"), axis=0).reshape(
        EXPERTS, ROWS, LANES
    )

    serves = y * 2 + tp // 2
    quarter = (tp % 2) * 2 + c
    at_home = (tp // 2 == c).astype(jnp.int32)
    numbers = jnp.stack([z, z * PLANES + serves, quarter, at_home]).astype(jnp.int32)
    codes = chosen_rows(numbers, code_all)
    outgoing = expand(numbers, code_column, column_states)
    outgoing, *seconds = tied(outgoing, *seconds)
    parts = []
    for own, first, second in zip(owns, firsts, seconds, strict=True):
        parts += [
            own,
            first,
            lax.ppermute(own, PAIR, out_of_home),
            second,
            lax.ppermute(first, PAIR, both),
            lax.ppermute(second, PAIR, to_home),
        ]
    plane = ("y", "c", "tp")
    arrived = lax.all_to_all(outgoing, plane, split_axis=0, concat_axis=0, tiled=True)

    groups = jnp.arange(EXPERTS, dtype=jnp.int32)
    inverse = jnp.sum(
        jnp.where(group_order[None, :] == groups[:, None], groups[None, :], 0), axis=1
    )
    source = inverse.reshape(PLANES, PLANES).T
    source_z, source_column = source // PLANES, source % PLANES
    distance = (source_z - z + PLANES) % PLANES
    position = jnp.zeros_like(distance)
    for spot_here, near in enumerate(NEAR):
        position = jnp.where(distance == near % PLANES, spot_here, position)
    origin = (source_column * PLANES + position)[:, :, None] * QUARTER + jnp.arange(
        QUARTER, dtype=jnp.int32
    )
    result = expert(
        numbers,
        arrived.reshape(PLANES, TP, 64, COLS),
        codes,
        origin.reshape(512, 1),
        post_gain[None],
        router.T,
        parts,
    )
    answers = lax.all_to_all(
        result.reshape(32, 64, COLS), plane, split_axis=0, concat_axis=0, tiled=True
    )
    mine = lax.dynamic_index_in_dim(source, column, 0, keepdims=False)
    rows_in_code = (mine % PLANES) * PLANES + mine // PLANES
    sums = combine(numbers, rows_in_code, code_all, answers)
    return lax.psum_scatter(
        sums.reshape(PLANES * ROWS, COLS), "z", scatter_dimension=0, tiled=True
    )


def solution(mesh):
    split = Mesh(mesh.devices.reshape(PLANES, 4, 2, TP), ("z", "y", "c", "tp"))
    req = ("z", "y", "c")
    return jax.shard_map(
        per_device,
        mesh=split,
        in_specs=(
            P(req, None, "tp"),
            P(req, None),
            P("tp"),
            P("tp"),
            P(req, None, None, "tp"),
            P(req, None, None, "tp"),
            P(req),
            P(req),
            P(),
            P(req, None),
            P("tp", None),
            P(),
            P(),
            P(req, None, "tp"),
            P(req, None, "tp"),
            P(req, "tp", None),
        ),
        out_specs=P(req, "tp"),
        check_vma=False,
    )
```

```python
import functools
import math

import jax
import jax.numpy as jnp
from jax import lax
from jax.experimental import pallas as pl
from jax.experimental.pallas import tpu as pltpu
from jax.sharding import Mesh, PartitionSpec as P

HEAD_DIM = 128
HEADS_HERE = 4
PRE = 128
DEC = 4
ROWS = PRE + DEC
PADDED = 136
SLOTS = 512
COLS = 512
FULL = 2048
EXPERTS = 64
LANES = 128
CAP = 32
PLANES = 8
TP = 4
QUARTER = 8
PAIR_LANES = 512
VMEM_LIMIT = 56 * 1024 * 1024
NEAR = (0, -1, 1, -2, 2, -3, 3, 4)
BF = jnp.bfloat16
F32 = jnp.float32
VM = pl.BlockSpec(memory_space=pltpu.VMEM)
SM = pl.BlockSpec(memory_space=pltpu.SMEM)
HB = pl.BlockSpec(memory_space=pl.ANY)


def dot(a, b, contract_a=1, contract_b=0):
    return lax.dot_general(
        a, b, (((contract_a,), (contract_b,)), ((), ())), preferred_element_type=F32
    )


def iota(shape, axis):
    return lax.broadcasted_iota(jnp.int32, shape, axis)


def attention_kernel(
    numbers, proj, inv, cosine, sine, q_gain, k_gain, context, cache, weight, own, *rest
):
    sends, total = rest[:3], rest[3]
    head = pl.program_id(0)
    factor = 1.0 / math.sqrt(HEAD_DIM)
    cos_v, sin_v = cosine[...], sine[...]

    def rotated(part, gain, column):
        norm = proj[part].astype(F32) * inv[:, column : column + 1] * gain[...]
        return (norm * cos_v + pltpu.roll(norm, HEAD_DIM // 2, 1) * sin_v).astype(BF)

    qr = rotated(0, q_gain, 0)
    kr = rotated(1, k_gain, 1)
    value = proj[2]
    low = jnp.finfo(F32).min

    q_pre, k_pre, v_pre = qr[:PRE], kr[:PRE], value[:PRE]
    rows = context.reshape(2 * SLOTS, HEAD_DIM)[...]
    column = iota((PRE, 2 * SLOTS), 1)
    seen = ((column & 1) == 0) & (column < 2 * numbers[0])
    s_old = jnp.where(seen, dot(q_pre, rows, 1, 1) * factor, low)
    causal = iota((PRE, PRE), 1) <= iota((PRE, PRE), 0)
    s_new = jnp.where(causal, dot(q_pre, k_pre, 1, 1) * factor, low)
    top = jnp.maximum(
        jnp.max(s_old, axis=1, keepdims=True), jnp.max(s_new, axis=1, keepdims=True)
    )
    e_old = jnp.where(seen, jnp.exp(s_old - top), 0.0)
    e_new = jnp.where(causal, jnp.exp(s_new - top), 0.0)
    share = 1.0 / (
        jnp.sum(e_old, axis=1, keepdims=True) + jnp.sum(e_new, axis=1, keepdims=True)
    )
    p_old = pltpu.roll(e_old * share, 1, 1).astype(BF)
    p_new = (e_new * share).astype(BF)
    mixed_pre = (dot(p_old, rows) + dot(p_new, v_pre)).astype(BF)

    q_dec, k_dec, v_dec = qr[PRE:], kr[PRE:], value[PRE:]
    keys = cache.reshape(DEC * 2 * SLOTS, HEAD_DIM)[...]
    row = iota((DEC, DEC * 2 * SLOTS), 0)
    column = iota((DEC, DEC * 2 * SLOTS), 1)
    length = jnp.where(
        row == 0,
        numbers[1],
        jnp.where(row == 1, numbers[2], jnp.where(row == 2, numbers[3], numbers[4])),
    )
    place = column - row * (2 * SLOTS)
    seen = ((column & 1) == 0) & (place >= 0) & (place < 2 * length)
    s_old = jnp.where(seen, dot(q_dec, keys, 1, 1) * factor, low)
    s_own = (
        jnp.sum(q_dec.astype(F32) * k_dec.astype(F32), axis=1, keepdims=True) * factor
    )
    top = jnp.maximum(jnp.max(s_old, axis=1, keepdims=True), s_own)
    e_old = jnp.where(seen, jnp.exp(s_old - top), 0.0)
    e_own = jnp.exp(s_own - top)
    share = 1.0 / (jnp.sum(e_old, axis=1, keepdims=True) + e_own)
    p_old = pltpu.roll(e_old * share, 1, 1).astype(BF)
    p_own = (e_own * share).astype(BF).astype(F32)
    mixed_dec = (dot(p_old, keys) + p_own * v_dec.astype(F32)).astype(BF)

    w = weight[...]
    out_pre = dot(mixed_pre, w)
    out_dec = dot(mixed_dec, w)

    @pl.when(head == 0)
    def _():
        for block in range(TP):
            span = slice(block * COLS, (block + 1) * COLS)
            total[block, :PRE] = out_pre[:, span]
            total[block, PRE:] = out_dec[:, span]

    @pl.when(head > 0)
    def _():
        for block in range(TP):
            span = slice(block * COLS, (block + 1) * COLS)
            total[block, :PRE] += out_pre[:, span]
            total[block, PRE:] += out_dec[:, span]

    @pl.when(head == HEADS_HERE - 1)
    def _():
        own[...] = total[numbers[5]]
        for step in range(1, TP):
            sends[step - 1][...] = total[(numbers[5] + step) % TP].astype(BF)


def attention(numbers, proj, inv, cosine, sine, q_gain, k_gain, context, cache, weight):
    whole = lambda *shape: pl.BlockSpec(shape, lambda h: (0,) * len(shape))
    return pl.pallas_call(
        attention_kernel,
        grid=(HEADS_HERE,),
        in_specs=[
            SM,
            pl.BlockSpec((3, ROWS, HEAD_DIM), lambda h: (0, 0, h)),
            whole(ROWS, 2),
            whole(ROWS, HEAD_DIM),
            whole(ROWS, HEAD_DIM),
            pl.BlockSpec((1, HEAD_DIM), lambda h: (0, h)),
            pl.BlockSpec((1, HEAD_DIM), lambda h: (0, h)),
            pl.BlockSpec((1, SLOTS, 2, HEAD_DIM), lambda h: (0, 0, 0, h)),
            pl.BlockSpec((DEC, SLOTS, 2, HEAD_DIM), lambda h: (0, 0, 0, h)),
            pl.BlockSpec((HEAD_DIM, FULL), lambda h: (h, 0)),
        ],
        out_specs=[whole(ROWS, COLS)] * TP,
        out_shape=[jax.ShapeDtypeStruct((ROWS, COLS), F32)]
        + [jax.ShapeDtypeStruct((ROWS, COLS), BF)] * (TP - 1),
        scratch_shapes=[pltpu.VMEM((TP, ROWS, COLS), F32)],
        compiler_params=pltpu.CompilerParams(vmem_limit_bytes=VMEM_LIMIT),
        cost_estimate=pl.CostEstimate(
            flops=2_000_000_000, bytes_accessed=10_000_000, transcendentals=1_000_000
        ),
        name="attention",
    )(numbers, proj, inv, cosine, sine, q_gain, k_gain, context, cache, weight)


def slot_part(code):
    wide = code.astype(F32)
    return jnp.where(wide > 64.0, wide - 64.0, wide)


def pair_onehot(code, plane, second):
    place = iota((LANES, PAIR_LANES), 1)
    device = place >> 4
    x, c, y = device & 3, (device >> 2) & 1, device >> 3
    expert = plane * PLANES + y * 2 + (x >> 1)
    spread = (iota((LANES, PAIR_LANES), 0) == expert).astype(F32).astype(BF)
    slot = dot(slot_part(code).astype(BF), spread)
    place = iota((1, PAIR_LANES), 1)
    device = place >> 4
    quarter = (device & 1) * 2 + ((device >> 2) & 1)
    wanted = quarter * QUARTER + (place & 7) + 1
    wanted = jnp.where(((place >> 3) & 1) == second, wanted, -1).astype(F32)
    return (slot == wanted).astype(F32).astype(BF)


def hits_kernel(numbers, order, code, out):
    for position in range(PLANES):
        out[position] = pair_onehot(
            code[order[position]][:ROWS], numbers[0], position & 1
        )


def pair_hits(numbers, order, code):
    return pl.pallas_call(
        hits_kernel,
        in_specs=[SM, SM, VM],
        out_specs=VM,
        out_shape=jax.ShapeDtypeStruct((PLANES, ROWS, PAIR_LANES), BF),
        compiler_params=pltpu.CompilerParams(vmem_limit_bytes=VMEM_LIMIT),
        cost_estimate=pl.CostEstimate(
            flops=700_000_000, bytes_accessed=4_000_000, transcendentals=0
        ),
        name="pair_hits",
    )(numbers, order, code)


def expand_kernel(hits, *refs):
    held, out = refs[:-1], refs[-1]
    for pair in range(PLANES // 2):
        filled = None
        for second in range(2):
            position = 2 * pair + second
            if position < PLANES - 1:
                rows = held[position][...]
            else:
                rows = jnp.concatenate(
                    [held[position][...], held[position + 1][...]], axis=0
                )
            part = dot(hits[position], rows, 0, 0)
            filled = part if filled is None else filled + part
        out[:, 16 * pair : 16 * pair + 16, :] = filled.astype(BF).reshape(32, 16, COLS)


def expand(hits, held):
    return pl.pallas_call(
        expand_kernel,
        in_specs=[VM] * (1 + len(held)),
        out_specs=VM,
        out_shape=jax.ShapeDtypeStruct((32, 64, COLS), BF),
        compiler_params=pltpu.CompilerParams(vmem_limit_bytes=VMEM_LIMIT),
        cost_estimate=pl.CostEstimate(
            flops=700_000_000, bytes_accessed=4_000_000, transcendentals=0
        ),
        name="expand",
    )(hits, *held)


def combine_kernel(hits, answers, out):
    rows = answers[...].reshape(PAIR_LANES, COLS)
    for second in range(2):
        out[second] = dot(hits[second], rows).astype(BF)


def combine(hits, answers):
    return pl.pallas_call(
        combine_kernel,
        grid=(PLANES // 2,),
        in_specs=[
            pl.BlockSpec((2, ROWS, PAIR_LANES), lambda p: (p, 0, 0)),
            pl.BlockSpec((32, 16, COLS), lambda p: (0, p, 0)),
        ],
        out_specs=pl.BlockSpec((2, ROWS, COLS), lambda p: (p, 0, 0)),
        out_shape=jax.ShapeDtypeStruct((PLANES, ROWS, COLS), BF),
        compiler_params=pltpu.CompilerParams(vmem_limit_bytes=VMEM_LIMIT),
        cost_estimate=pl.CostEstimate(
            flops=600_000_000, bytes_accessed=4_000_000, transcendentals=0
        ),
        name="combine",
    )(hits, answers)


def chosen_kernel(numbers, code, out):
    plane, expert, quarter = numbers[0], numbers[1], numbers[2]
    is_expert = iota((ROWS, LANES), 1) == expert
    place = iota((1, 64), 1)
    wanted = quarter * QUARTER + (place & 7) + 1

    def one(column, carry):
        filled = jnp.zeros((64, LANES), F32)
        for position in range(PLANES):
            z = (plane + NEAR[position] + PLANES) % PLANES
            rows = code[column * PLANES + z][:ROWS]
            slot = jnp.sum(
                jnp.where(is_expert, slot_part(rows), 0.0), axis=1, keepdims=True
            )
            aim = jnp.where((place >> 3) == position, wanted, -1).astype(F32)
            hits = (slot == aim).astype(F32).astype(BF)
            filled = filled + dot(hits, rows, 0, 0)
        out[column] = filled
        return carry

    lax.fori_loop(0, PLANES, one, 0)


def chosen_rows(numbers, code):
    return pl.pallas_call(
        chosen_kernel,
        in_specs=[SM, VM],
        out_specs=VM,
        out_shape=jax.ShapeDtypeStruct((PLANES, 64, LANES), F32),
        compiler_params=pltpu.CompilerParams(vmem_limit_bytes=VMEM_LIMIT),
        cost_estimate=pl.CostEstimate(
            flops=200_000_000, bytes_accessed=2_000_000, transcendentals=0
        ),
        name="chosen_rows",
    )(numbers, code)


def weight_copies(parts, target, sems, at_home, begin):
    own, first, other_own, second, other_first, other_second = parts
    if not begin:
        for quarter in range(4):
            pltpu.make_async_copy(
                target(first), target(None, quarter), sems.at[quarter]
            ).wait()
        return

    def bring(source, quarter):
        pltpu.make_async_copy(
            target(source), target(None, quarter), sems.at[quarter]
        ).start()

    @pl.when(at_home == 1)
    def _():
        bring(own, 0)
        bring(other_second, 3)

    @pl.when(at_home == 0)
    def _():
        bring(other_own, 0)
        bring(second, 3)

    bring(first, 1)
    bring(other_first, 2)


def expert_kernel(numbers, arrived, codes, origin, gain, router, *refs):
    wide_parts, down_parts, out = refs[:6], refs[6:12], refs[12]
    wide, down, normed, hidden, sems = refs[13:18]
    at_home = numbers[3]
    to_wide = lambda source, quarter=None: wide.at[quarter] if source is None else source
    to_down = lambda source, quarter=None: (
        down.at[quarter * 256 : (quarter + 1) * 256] if source is None else source
    )
    weight_copies(wide_parts, to_wide, sems.at[0], at_home, True)
    weight_copies(down_parts, to_down, sems.at[1], at_home, True)

    squares = jnp.zeros((512, 1), F32)
    for x in range(TP):
        part = arrived[:, x].reshape(512, COLS).astype(F32)
        squares = squares + jnp.sum(part * part, axis=1, keepdims=True)
    scale = lax.rsqrt(squares / FULL + 1e-05)
    for x in range(TP):
        span = slice(x * COLS, (x + 1) * COLS)
        normed[:, span] = (arrived[:, x].reshape(512, COLS).astype(F32) * scale * gain[:, span]).astype(BF)
    logits = dot(normed[...], router[...], 1, 1)
    code = codes[...].reshape(512, LANES)[:, :EXPERTS]
    chosen = code > 0.0
    is_expert = iota((512, EXPERTS), 1) == numbers[1]
    top = jnp.max(jnp.where(chosen, logits, jnp.finfo(F32).min), axis=1, keepdims=True)
    raised = jnp.where(chosen, jnp.exp(jnp.minimum(logits - top, 0.0)), 0.0)
    bottom = jnp.sum(raised, axis=1, keepdims=True)
    share = jnp.sum(jnp.where(is_expert, raised, 0.0), axis=1, keepdims=True)
    gate = jnp.where(bottom > 0.0, share / jnp.where(bottom > 0.0, bottom, 1.0), 0.0)
    mark = jnp.sum(jnp.where(is_expert, code, 0.0), axis=1, keepdims=True)
    first_choice = (mark > 64.0).astype(F32)

    weight_copies(wide_parts, to_wide, sems.at[0], at_home, False)
    for quarter in range(4):
        gate_pre = dot(normed[...], wide[quarter, :FULL])
        up_pre = dot(normed[...], wide[quarter, FULL:])
        hidden[:, quarter * 256 : (quarter + 1) * 256] = (
            gate_pre / (1.0 + jnp.exp(-gate_pre)) * up_pre
        ).astype(BF)
    weight_copies(down_parts, to_down, sems.at[1], at_home, False)
    move = (origin[...] == iota((512, 512), 1)).astype(F32).astype(BF)
    for x in range(TP):
        span = slice(x * COLS, (x + 1) * COLS)
        part = arrived[:, x].reshape(512, COLS).astype(F32)
        result = dot(hidden[...], down[:, span]).astype(BF).astype(F32) * gate
        piece = (result + first_choice * part).astype(BF)
        out[:, x] = dot(move, piece).astype(BF).reshape(PLANES, 64, COLS)


def expert(numbers, arrived, codes, origin, gain, router, wide_parts, down_parts):
    return pl.pallas_call(
        expert_kernel,
        in_specs=[SM] + [VM] * 5 + [HB] * 12,
        out_specs=VM,
        out_shape=jax.ShapeDtypeStruct((PLANES, TP, 64, COLS), BF),
        scratch_shapes=[
            pltpu.VMEM((4, 2 * FULL, 256), BF),
            pltpu.VMEM((1024, FULL), BF),
            pltpu.VMEM((512, FULL), BF),
            pltpu.VMEM((512, 1024), BF),
            pltpu.SemaphoreType.DMA((2, 4)),
        ],
        compiler_params=pltpu.CompilerParams(vmem_limit_bytes=VMEM_LIMIT),
        cost_estimate=pl.CostEstimate(
            flops=8_000_000_000, bytes_accessed=20_000_000, transcendentals=500_000
        ),
        name="expert",
    )(numbers, arrived, codes, origin, gain, router, *wide_parts, *down_parts)


def pair_moves():
    at = lambda core, x: core * TP + x
    over = lambda d: (d + TP) % (2 * TP)
    first = [
        (at(0, 0), at(0, 1)),
        (at(0, 1), at(0, 0)),
        (at(0, 2), at(1, 1)),
        (at(0, 3), at(1, 0)),
        (at(1, 2), at(1, 3)),
        (at(1, 3), at(1, 2)),
        (at(1, 1), at(0, 2)),
        (at(1, 0), at(0, 3)),
    ]
    second = [
        (at(1, 0), at(1, 1)),
        (at(1, 1), at(1, 0)),
        (at(0, 2), at(0, 3)),
        (at(0, 3), at(0, 2)),
    ]
    home = [at(0, 0), at(0, 1), at(1, 2), at(1, 3)]
    return (
        first,
        second,
        [(d, over(d)) for d in home],
        [(d, over(d)) for d in range(2 * TP)],
        [(over(d), d) for d in home],
    )


PAIR = ("c", "tp")


def tied(*values):
    return lax.optimization_barrier(values)


def around(value, axis, step):
    count = lax.axis_size(axis)
    return lax.ppermute(value, axis, [(i, (i + step) % count) for i in range(count)])


def per_device(
    projected,
    residual,
    query_gain,
    key_gain,
    context_cache,
    decode_cache,
    offsets,
    lengths,
    group_order,
    expert_ids,
    out_weight,
    post_gain,
    router,
    gate_weight,
    up_weight,
    down_weight,
):
    z, y, c, tp = (lax.axis_index(name) for name in ("z", "y", "c", "tp"))
    column = y * 2 + c

    every = jnp.arange(LANES, dtype=jnp.int32)
    chosen = jnp.zeros((ROWS, LANES), jnp.bool_)
    for k in range(expert_ids.shape[1]):
        chosen = chosen | (expert_ids[:, k : k + 1] == every[None, :])
    below = jnp.arange(ROWS)[:, None] >= jnp.arange(ROWS)[None, :]
    slot = dot(below.astype(BF), chosen.astype(BF))
    first_choice = expert_ids[:, :1] == every[None, :]
    code = jnp.where(chosen, slot + 64.0 * first_choice, 0.0).astype(BF)
    widened = jnp.pad(code, ((0, PADDED - ROWS), (0, COLS - LANES)))
    code_column = lax.all_gather(widened, "z", axis=0)

    first_move, second_move, out_of_home, both, to_home = pair_moves()
    wide = jnp.concatenate([gate_weight[0], up_weight[0]], axis=0)
    down = down_weight[0]

    proj = jnp.transpose(projected, (1, 0, 2))
    raw = proj[:2].astype(F32)
    squares = jnp.sum(raw * raw, axis=2)
    shared = [around(squares, "tp", step) for step in range(1, TP)]
    squares = squares + shared[0] + shared[1] + shared[2]
    squares, wide = tied(squares, wide)
    wide_first = lax.ppermute(wide, PAIR, first_move)
    inv = lax.rsqrt(squares / FULL + 1e-05).T
    spot = jnp.arange(ROWS, dtype=jnp.int32)
    positions = offsets[0] + spot
    for i in range(DEC):
        positions = jnp.where(spot == PRE + i, lengths[i], positions)
    half = HEAD_DIM // 2
    frequency = 10000.0 ** (-2.0 * jnp.arange(half, dtype=F32) / HEAD_DIM)
    angles = positions.astype(F32)[:, None] * frequency[None, :]
    cosine, sine = jnp.cos(angles), jnp.sin(angles)
    cosine = jnp.concatenate([cosine, cosine], axis=1)
    sine = jnp.concatenate([-sine, sine], axis=1)
    numbers = jnp.concatenate([offsets, lengths, tp[None].astype(jnp.int32)])
    own, *sends = attention(
        numbers,
        proj,
        inv,
        cosine,
        sine,
        query_gain[None],
        key_gain[None],
        context_cache,
        decode_cache,
        out_weight,
    )
    *sends, wide_first = tied(*sends, wide_first)
    state = own
    for step in range(1, TP):
        state = state + around(sends[step - 1], "tp", step).astype(F32)
    residual_here = lax.dynamic_slice_in_dim(residual, tp * COLS, COLS, 1)
    state = (residual_here.astype(F32) + state).astype(BF)
    serves = y * 2 + tp // 2
    quarter = (tp % 2) * 2 + c
    at_home = (tp // 2 == c).astype(jnp.int32)
    numbers = jnp.stack([z, z * PLANES + serves, quarter, at_home]).astype(jnp.int32)

    state, wide_first, down = tied(state, wide_first, down)
    down_first = lax.ppermute(down, PAIR, first_move)
    wide_second = lax.ppermute(wide_first, PAIR, second_move)

    up_1, down_1 = around(state, "z", 1), around(state, "z", -1)
    up_2, down_2 = around(up_1, "z", 1), around(down_1, "z", -1)
    up_2, down_2, code_column = tied(up_2, down_2, code_column)
    code_column = code_column[:, :, :LANES]
    code_all = lax.all_gather(code_column, ("y", "c"), axis=0).reshape(
        EXPERTS, PADDED, LANES
    )
    near = (z + jnp.array(NEAR, jnp.int32) + PLANES) % PLANES
    out_hits = pair_hits(numbers, near.astype(jnp.int32), code_column)
    plane = ("y", "c", "tp")

    def exchanged(blocks):
        return lax.all_to_all(blocks, plane, split_axis=0, concat_axis=0, tiled=True)

    up_3, down_3 = around(up_2, "z", 1), around(down_2, "z", -1)
    far = [around(up_3[:64], "z", 1), around(down_3[64:], "z", -1)]
    *far, down_first = tied(*far, down_first)
    down_second = lax.ppermute(down_first, PAIR, second_move)
    outgoing = expand(out_hits, [state, up_1, down_1, up_2, down_2, up_3, down_3, *far])
    outgoing, wide_second = tied(outgoing, wide_second)
    arrived = exchanged(outgoing)
    codes = chosen_rows(numbers, code_all)

    groups = jnp.arange(EXPERTS, dtype=jnp.int32)
    inverse = jnp.sum(
        jnp.where(group_order[None, :] == groups[:, None], groups[None, :], 0), axis=1
    )
    source = inverse.reshape(PLANES, PLANES).T
    source_z, source_column = source // PLANES, source % PLANES
    distance = (source_z - z + PLANES) % PLANES
    position = jnp.zeros_like(distance)
    for spot_here, near in enumerate(NEAR):
        position = jnp.where(distance == near % PLANES, spot_here, position)
    origin = (source_column * PLANES + position)[:, :, None] * QUARTER + jnp.arange(
        QUARTER, dtype=jnp.int32
    )
    mine = lax.dynamic_index_in_dim(source, column, 0, keepdims=False)
    back_hits = pair_hits(numbers, (mine % PLANES) * PLANES + mine // PLANES, code_all)
    codes, back_hits = tied(codes, back_hits)
    wide_parts, down_parts = (
        [
            own,
            first,
            lax.ppermute(own, PAIR, out_of_home),
            second,
            lax.ppermute(first, PAIR, both),
            lax.ppermute(second, PAIR, to_home),
        ]
        for own, first, second in (
            (wide, wide_first, wide_second),
            (down, down_first, down_second),
        )
    )
    result = expert(
        numbers,
        arrived.reshape(PLANES, TP, 64, COLS),
        codes,
        origin.reshape(512, 1),
        post_gain[None],
        router.T,
        wide_parts,
        down_parts,
    )
    answers = exchanged(result.reshape(32, 64, COLS))
    sums = combine(back_hits, answers).reshape(PLANES * ROWS, COLS)
    return lax.psum_scatter(sums, "z", scatter_dimension=0, tiled=True)


def solution(mesh):
    split = Mesh(mesh.devices.reshape(PLANES, 4, 2, TP), ("z", "y", "c", "tp"))
    req = ("z", "y", "c")
    return jax.shard_map(
        per_device,
        mesh=split,
        in_specs=(
            P(req, None, "tp"),
            P(req, None),
            P("tp"),
            P("tp"),
            P(req, None, None, "tp"),
            P(req, None, None, "tp"),
            P(req),
            P(req),
            P(),
            P(req, None),
            P("tp", None),
            P(),
            P(),
            P(req, None, "tp"),
            P(req, None, "tp"),
            P(req, "tp", None),
        ),
        out_specs=P(req, "tp"),
        check_vma=False,
    )
```

```python
import functools
import math

import jax
import jax.numpy as jnp
from jax import lax
from jax.experimental import pallas as pl
from jax.experimental.pallas import tpu as pltpu
from jax.sharding import Mesh, PartitionSpec as P

HEAD_DIM = 128
HEADS_HERE = 4
PRE = 128
DEC = 4
ROWS = PRE + DEC
PADDED = 136
SLOTS = 512
COLS = 512
FULL = 2048
EXPERTS = 64
LANES = 128
CAP = 32
PLANES = 8
TP = 4
QUARTER = 8
PAIR_LANES = 512
VMEM_LIMIT = 56 * 1024 * 1024
NEAR = (0, -1, 1, -2, 2, -3, 3, 4)
BF = jnp.bfloat16
F32 = jnp.float32
VM = pl.BlockSpec(memory_space=pltpu.VMEM)
SM = pl.BlockSpec(memory_space=pltpu.SMEM)
HB = pl.BlockSpec(memory_space=pl.ANY)


def dot(a, b, contract_a=1, contract_b=0):
    return lax.dot_general(
        a, b, (((contract_a,), (contract_b,)), ((), ())), preferred_element_type=F32
    )


def iota(shape, axis):
    return lax.broadcasted_iota(jnp.int32, shape, axis)


def attention_kernel(
    numbers, proj, inv, cosine, sine, q_gain, k_gain, context, cache, weight, own, *rest
):
    sends, total = rest[:3], rest[3]
    head = pl.program_id(0)
    factor = 1.0 / math.sqrt(HEAD_DIM)
    cos_v, sin_v = cosine[...], sine[...]

    def rotated(part, gain, column):
        norm = proj[part].astype(F32) * inv[:, column : column + 1] * gain[...]
        return (norm * cos_v + pltpu.roll(norm, HEAD_DIM // 2, 1) * sin_v).astype(BF)

    qr = rotated(0, q_gain, 0)
    kr = rotated(1, k_gain, 1)
    value = proj[2]
    low = jnp.finfo(F32).min

    q_pre, k_pre, v_pre = qr[:PRE], kr[:PRE], value[:PRE]
    rows = context.reshape(2 * SLOTS, HEAD_DIM)[...]
    column = iota((PRE, 2 * SLOTS), 1)
    seen = ((column & 1) == 0) & (column < 2 * numbers[0])
    s_old = jnp.where(seen, dot(q_pre, rows, 1, 1) * factor, low)
    causal = iota((PRE, PRE), 1) <= iota((PRE, PRE), 0)
    s_new = jnp.where(causal, dot(q_pre, k_pre, 1, 1) * factor, low)
    top = jnp.maximum(
        jnp.max(s_old, axis=1, keepdims=True), jnp.max(s_new, axis=1, keepdims=True)
    )
    e_old = jnp.where(seen, jnp.exp(s_old - top), 0.0)
    e_new = jnp.where(causal, jnp.exp(s_new - top), 0.0)
    share = 1.0 / (
        jnp.sum(e_old, axis=1, keepdims=True) + jnp.sum(e_new, axis=1, keepdims=True)
    )
    p_old = pltpu.roll(e_old * share, 1, 1).astype(BF)
    p_new = (e_new * share).astype(BF)
    mixed_pre = (dot(p_old, rows) + dot(p_new, v_pre)).astype(BF)

    q_dec, k_dec, v_dec = qr[PRE:], kr[PRE:], value[PRE:]
    keys = cache.reshape(DEC * 2 * SLOTS, HEAD_DIM)[...]
    row = iota((DEC, DEC * 2 * SLOTS), 0)
    column = iota((DEC, DEC * 2 * SLOTS), 1)
    length = jnp.where(
        row == 0,
        numbers[1],
        jnp.where(row == 1, numbers[2], jnp.where(row == 2, numbers[3], numbers[4])),
    )
    place = column - row * (2 * SLOTS)
    seen = ((column & 1) == 0) & (place >= 0) & (place < 2 * length)
    s_old = jnp.where(seen, dot(q_dec, keys, 1, 1) * factor, low)
    s_own = (
        jnp.sum(q_dec.astype(F32) * k_dec.astype(F32), axis=1, keepdims=True) * factor
    )
    top = jnp.maximum(jnp.max(s_old, axis=1, keepdims=True), s_own)
    e_old = jnp.where(seen, jnp.exp(s_old - top), 0.0)
    e_own = jnp.exp(s_own - top)
    share = 1.0 / (jnp.sum(e_old, axis=1, keepdims=True) + e_own)
    p_old = pltpu.roll(e_old * share, 1, 1).astype(BF)
    p_own = (e_own * share).astype(BF).astype(F32)
    mixed_dec = (dot(p_old, keys) + p_own * v_dec.astype(F32)).astype(BF)

    w = weight[...]
    out_pre = dot(mixed_pre, w)
    out_dec = dot(mixed_dec, w)

    @pl.when(head == 0)
    def _():
        for block in range(TP):
            span = slice(block * COLS, (block + 1) * COLS)
            total[block, :PRE] = out_pre[:, span]
            total[block, PRE:] = out_dec[:, span]

    @pl.when(head > 0)
    def _():
        for block in range(TP):
            span = slice(block * COLS, (block + 1) * COLS)
            total[block, :PRE] += out_pre[:, span]
            total[block, PRE:] += out_dec[:, span]

    @pl.when(head == HEADS_HERE - 1)
    def _():
        own[...] = total[numbers[5]]
        for step in range(1, TP):
            sends[step - 1][...] = total[(numbers[5] + step) % TP].astype(BF)


def attention(numbers, proj, inv, cosine, sine, q_gain, k_gain, context, cache, weight):
    whole = lambda *shape: pl.BlockSpec(shape, lambda h: (0,) * len(shape))
    return pl.pallas_call(
        attention_kernel,
        grid=(HEADS_HERE,),
        in_specs=[
            SM,
            pl.BlockSpec((3, ROWS, HEAD_DIM), lambda h: (0, 0, h)),
            whole(ROWS, 2),
            whole(ROWS, HEAD_DIM),
            whole(ROWS, HEAD_DIM),
            pl.BlockSpec((1, HEAD_DIM), lambda h: (0, h)),
            pl.BlockSpec((1, HEAD_DIM), lambda h: (0, h)),
            pl.BlockSpec((1, SLOTS, 2, HEAD_DIM), lambda h: (0, 0, 0, h)),
            pl.BlockSpec((DEC, SLOTS, 2, HEAD_DIM), lambda h: (0, 0, 0, h)),
            pl.BlockSpec((HEAD_DIM, FULL), lambda h: (h, 0)),
        ],
        out_specs=[whole(ROWS, COLS)] * TP,
        out_shape=[jax.ShapeDtypeStruct((ROWS, COLS), F32)]
        + [jax.ShapeDtypeStruct((ROWS, COLS), BF)] * (TP - 1),
        scratch_shapes=[pltpu.VMEM((TP, ROWS, COLS), F32)],
        compiler_params=pltpu.CompilerParams(vmem_limit_bytes=VMEM_LIMIT),
        cost_estimate=pl.CostEstimate(
            flops=2_000_000_000, bytes_accessed=10_000_000, transcendentals=1_000_000
        ),
        name="attention",
    )(numbers, proj, inv, cosine, sine, q_gain, k_gain, context, cache, weight)


def slot_part(code):
    wide = code.astype(F32)
    return jnp.where(wide > 64.0, wide - 64.0, wide)


def pair_onehot(code, plane, second):
    place = iota((LANES, PAIR_LANES), 1)
    device = place >> 4
    x, c, y = device & 3, (device >> 2) & 1, device >> 3
    expert = plane * PLANES + y * 2 + (x >> 1)
    spread = (iota((LANES, PAIR_LANES), 0) == expert).astype(F32).astype(BF)
    slot = dot(slot_part(code).astype(BF), spread)
    place = iota((1, PAIR_LANES), 1)
    device = place >> 4
    quarter = (device & 1) * 2 + ((device >> 2) & 1)
    wanted = quarter * QUARTER + (place & 7) + 1
    wanted = jnp.where(((place >> 3) & 1) == second, wanted, -1).astype(F32)
    return (slot == wanted).astype(F32).astype(BF)


def hits_kernel(numbers, order, code, out):
    for position in range(PLANES):
        out[position] = pair_onehot(
            code[order[position]][:ROWS], numbers[0], position & 1
        )


def pair_hits(numbers, order, code):
    return pl.pallas_call(
        hits_kernel,
        in_specs=[SM, SM, VM],
        out_specs=VM,
        out_shape=jax.ShapeDtypeStruct((PLANES, ROWS, PAIR_LANES), BF),
        compiler_params=pltpu.CompilerParams(vmem_limit_bytes=VMEM_LIMIT),
        cost_estimate=pl.CostEstimate(
            flops=700_000_000, bytes_accessed=4_000_000, transcendentals=0
        ),
        name="pair_hits",
    )(numbers, order, code)


def expand_kernel(hits, *refs):
    held, out = refs[:-1], refs[-1]
    for pair in range(PLANES // 2):
        filled = None
        for second in range(2):
            position = 2 * pair + second
            if position < PLANES - 1:
                rows = held[position][...]
            else:
                rows = jnp.concatenate(
                    [held[position][...], held[position + 1][...]], axis=0
                )
            part = dot(hits[position], rows, 0, 0)
            filled = part if filled is None else filled + part
        out[:, 16 * pair : 16 * pair + 16, :] = filled.astype(BF).reshape(32, 16, COLS)


def expand(hits, held):
    return pl.pallas_call(
        expand_kernel,
        in_specs=[VM] * (1 + len(held)),
        out_specs=VM,
        out_shape=jax.ShapeDtypeStruct((32, 64, COLS), BF),
        compiler_params=pltpu.CompilerParams(vmem_limit_bytes=VMEM_LIMIT),
        cost_estimate=pl.CostEstimate(
            flops=700_000_000, bytes_accessed=4_000_000, transcendentals=0
        ),
        name="expand",
    )(hits, *held)


def combine_kernel(hits, answers, out):
    rows = answers[...].reshape(PAIR_LANES, COLS)
    for second in range(2):
        out[second] = dot(hits[second], rows).astype(BF)


def combine(hits, answers):
    return pl.pallas_call(
        combine_kernel,
        grid=(PLANES // 2,),
        in_specs=[
            pl.BlockSpec((2, ROWS, PAIR_LANES), lambda p: (p, 0, 0)),
            pl.BlockSpec((32, 16, COLS), lambda p: (0, p, 0)),
        ],
        out_specs=pl.BlockSpec((2, ROWS, COLS), lambda p: (p, 0, 0)),
        out_shape=jax.ShapeDtypeStruct((PLANES, ROWS, COLS), BF),
        compiler_params=pltpu.CompilerParams(vmem_limit_bytes=VMEM_LIMIT),
        cost_estimate=pl.CostEstimate(
            flops=600_000_000, bytes_accessed=4_000_000, transcendentals=0
        ),
        name="combine",
    )(hits, answers)


def chosen_kernel(numbers, code, out):
    plane, expert, quarter = numbers[0], numbers[1], numbers[2]
    is_expert = iota((ROWS, LANES), 1) == expert
    place = iota((1, 64), 1)
    wanted = quarter * QUARTER + (place & 7) + 1

    def one(column, carry):
        filled = jnp.zeros((64, LANES), F32)
        for position in range(PLANES):
            z = (plane + NEAR[position] + PLANES) % PLANES
            rows = code[column * PLANES + z][:ROWS]
            slot = jnp.sum(
                jnp.where(is_expert, slot_part(rows), 0.0), axis=1, keepdims=True
            )
            aim = jnp.where((place >> 3) == position, wanted, -1).astype(F32)
            hits = (slot == aim).astype(F32).astype(BF)
            filled = filled + dot(hits, rows, 0, 0)
        out[column] = filled
        return carry

    lax.fori_loop(0, PLANES, one, 0)


def chosen_rows(numbers, code):
    return pl.pallas_call(
        chosen_kernel,
        in_specs=[SM, VM],
        out_specs=VM,
        out_shape=jax.ShapeDtypeStruct((PLANES, 64, LANES), F32),
        compiler_params=pltpu.CompilerParams(vmem_limit_bytes=VMEM_LIMIT),
        cost_estimate=pl.CostEstimate(
            flops=200_000_000, bytes_accessed=2_000_000, transcendentals=0
        ),
        name="chosen_rows",
    )(numbers, code)


def await_quarter(parts, target, sems, quarter):
    pltpu.make_async_copy(parts[1], target(None, quarter), sems.at[quarter]).wait()


def bring_quarters(parts, target, sems, at_home):
    own, first, other_own, second, other_first, other_second = parts
    def bring(source, quarter):
        pltpu.make_async_copy(
            target(source), target(None, quarter), sems.at[quarter]
        ).start()

    @pl.when(at_home == 1)
    def _():
        bring(own, 0)
        bring(other_second, 3)

    @pl.when(at_home == 0)
    def _():
        bring(other_own, 0)
        bring(second, 3)

    bring(first, 1)
    bring(other_first, 2)


def expert_kernel(numbers, arrived, codes, origin, gain, router, *refs):
    wide_parts, down_parts, out = refs[:6], refs[6:12], refs[12]
    wide, down, normed, hidden, sems = refs[13:18]
    at_home = numbers[3]
    to_wide = lambda source, quarter=None: wide.at[quarter] if source is None else source
    to_down = lambda source, quarter=None: (
        down.at[quarter * 256 : (quarter + 1) * 256] if source is None else source
    )
    bring_quarters(wide_parts, to_wide, sems.at[0], at_home)
    bring_quarters(down_parts, to_down, sems.at[1], at_home)

    squares = jnp.zeros((512, 1), F32)
    for x in range(TP):
        part = arrived[:, x].reshape(512, COLS).astype(F32)
        squares = squares + jnp.sum(part * part, axis=1, keepdims=True)
    scale = lax.rsqrt(squares / FULL + 1e-05)
    for x in range(TP):
        span = slice(x * COLS, (x + 1) * COLS)
        normed[:, span] = (arrived[:, x].reshape(512, COLS).astype(F32) * scale * gain[:, span]).astype(BF)
    logits = dot(normed[...], router[...], 1, 1)
    code = codes[...].reshape(512, LANES)[:, :EXPERTS]
    chosen = code > 0.0
    is_expert = iota((512, EXPERTS), 1) == numbers[1]
    top = jnp.max(jnp.where(chosen, logits, jnp.finfo(F32).min), axis=1, keepdims=True)
    raised = jnp.where(chosen, jnp.exp(jnp.minimum(logits - top, 0.0)), 0.0)
    bottom = jnp.sum(raised, axis=1, keepdims=True)
    share = jnp.sum(jnp.where(is_expert, raised, 0.0), axis=1, keepdims=True)
    gate = jnp.where(bottom > 0.0, share / jnp.where(bottom > 0.0, bottom, 1.0), 0.0)
    mark = jnp.sum(jnp.where(is_expert, code, 0.0), axis=1, keepdims=True)
    first_choice = (mark > 64.0).astype(F32)

    for quarter in (0, 3, 1, 2):
        await_quarter(wide_parts, to_wide, sems.at[0], quarter)
        gate_pre = dot(normed[...], wide[quarter, :FULL])
        up_pre = dot(normed[...], wide[quarter, FULL:])
        hidden[:, quarter * 256 : (quarter + 1) * 256] = (
            gate_pre / (1.0 + jnp.exp(-gate_pre)) * up_pre
        ).astype(BF)
    for quarter in range(4):
        await_quarter(down_parts, to_down, sems.at[1], quarter)
    move = (origin[...] == iota((512, 512), 1)).astype(F32).astype(BF)
    for x in range(TP):
        span = slice(x * COLS, (x + 1) * COLS)
        part = arrived[:, x].reshape(512, COLS).astype(F32)
        result = dot(hidden[...], down[:, span]).astype(BF).astype(F32) * gate
        piece = (result + first_choice * part).astype(BF)
        out[:, x] = dot(move, piece).astype(BF).reshape(PLANES, 64, COLS)


def expert(numbers, arrived, codes, origin, gain, router, wide_parts, down_parts):
    return pl.pallas_call(
        expert_kernel,
        in_specs=[SM] + [VM] * 5 + [HB] * 12,
        out_specs=VM,
        out_shape=jax.ShapeDtypeStruct((PLANES, TP, 64, COLS), BF),
        scratch_shapes=[
            pltpu.VMEM((4, 2 * FULL, 256), BF),
            pltpu.VMEM((1024, FULL), BF),
            pltpu.VMEM((512, FULL), BF),
            pltpu.VMEM((512, 1024), BF),
            pltpu.SemaphoreType.DMA((2, 4)),
        ],
        compiler_params=pltpu.CompilerParams(vmem_limit_bytes=VMEM_LIMIT),
        cost_estimate=pl.CostEstimate(
            flops=8_000_000_000, bytes_accessed=20_000_000, transcendentals=500_000
        ),
        name="expert",
    )(numbers, arrived, codes, origin, gain, router, *wide_parts, *down_parts)


def pair_moves():
    at = lambda core, x: core * TP + x
    over = lambda d: (d + TP) % (2 * TP)
    first = [
        (at(0, 0), at(0, 1)),
        (at(0, 1), at(0, 0)),
        (at(0, 2), at(1, 1)),
        (at(0, 3), at(1, 0)),
        (at(1, 2), at(1, 3)),
        (at(1, 3), at(1, 2)),
        (at(1, 1), at(0, 2)),
        (at(1, 0), at(0, 3)),
    ]
    second = [
        (at(1, 0), at(1, 1)),
        (at(1, 1), at(1, 0)),
        (at(0, 2), at(0, 3)),
        (at(0, 3), at(0, 2)),
    ]
    home = [at(0, 0), at(0, 1), at(1, 2), at(1, 3)]
    return (
        first,
        second,
        [(d, over(d)) for d in home],
        [(d, over(d)) for d in range(2 * TP)],
        [(over(d), d) for d in home],
    )


PAIR = ("c", "tp")


def tied(*values):
    return lax.optimization_barrier(values)


def around(value, axis, step):
    count = lax.axis_size(axis)
    return lax.ppermute(value, axis, [(i, (i + step) % count) for i in range(count)])


def per_device(
    projected,
    residual,
    query_gain,
    key_gain,
    context_cache,
    decode_cache,
    offsets,
    lengths,
    group_order,
    expert_ids,
    out_weight,
    post_gain,
    router,
    gate_weight,
    up_weight,
    down_weight,
):
    z, y, c, tp = (lax.axis_index(name) for name in ("z", "y", "c", "tp"))
    column = y * 2 + c

    every = jnp.arange(LANES, dtype=jnp.int32)
    chosen = jnp.zeros((ROWS, LANES), jnp.bool_)
    for k in range(expert_ids.shape[1]):
        chosen = chosen | (expert_ids[:, k : k + 1] == every[None, :])
    below = jnp.arange(ROWS)[:, None] >= jnp.arange(ROWS)[None, :]
    slot = dot(below.astype(BF), chosen.astype(BF))
    first_choice = expert_ids[:, :1] == every[None, :]
    code = jnp.where(chosen, slot + 64.0 * first_choice, 0.0).astype(BF)
    widened = jnp.pad(code, ((0, PADDED - ROWS), (0, COLS - LANES)))
    code_column = lax.all_gather(widened, "z", axis=0)

    first_move, second_move, out_of_home, both, to_home = pair_moves()
    wide = jnp.concatenate([gate_weight[0], up_weight[0]], axis=0)
    down = down_weight[0]

    proj = jnp.transpose(projected, (1, 0, 2))
    raw = proj[:2].astype(F32)
    squares = jnp.sum(raw * raw, axis=2)
    shared = [around(squares, "tp", step) for step in range(1, TP)]
    squares = squares + shared[0] + shared[1] + shared[2]
    squares, wide = tied(squares, wide)
    wide_first = lax.ppermute(wide, PAIR, first_move)
    wide_other = lax.ppermute(wide, PAIR, out_of_home)
    down_other = lax.ppermute(down, PAIR, out_of_home)
    inv = lax.rsqrt(squares / FULL + 1e-05).T
    spot = jnp.arange(ROWS, dtype=jnp.int32)
    positions = offsets[0] + spot
    for i in range(DEC):
        positions = jnp.where(spot == PRE + i, lengths[i], positions)
    half = HEAD_DIM // 2
    frequency = 10000.0 ** (-2.0 * jnp.arange(half, dtype=F32) / HEAD_DIM)
    angles = positions.astype(F32)[:, None] * frequency[None, :]
    cosine, sine = jnp.cos(angles), jnp.sin(angles)
    cosine = jnp.concatenate([cosine, cosine], axis=1)
    sine = jnp.concatenate([-sine, sine], axis=1)
    numbers = jnp.concatenate([offsets, lengths, tp[None].astype(jnp.int32)])
    own, *sends = attention(
        numbers,
        proj,
        inv,
        cosine,
        sine,
        query_gain[None],
        key_gain[None],
        context_cache,
        decode_cache,
        out_weight,
    )
    *sends, wide_first, wide_other, down_other = tied(
        *sends, wide_first, wide_other, down_other
    )
    state = own
    for step in range(1, TP):
        state = state + around(sends[step - 1], "tp", step).astype(F32)
    residual_here = lax.dynamic_slice_in_dim(residual, tp * COLS, COLS, 1)
    state = (residual_here.astype(F32) + state).astype(BF)
    serves = y * 2 + tp // 2
    quarter = (tp % 2) * 2 + c
    at_home = (tp // 2 == c).astype(jnp.int32)
    numbers = jnp.stack([z, z * PLANES + serves, quarter, at_home]).astype(jnp.int32)

    state, wide_first, down = tied(state, wide_first, down)
    down_first = lax.ppermute(down, PAIR, first_move)
    wide_second = lax.ppermute(wide_first, PAIR, second_move)

    up_1, down_1 = around(state, "z", 1), around(state, "z", -1)
    up_2, down_2 = around(up_1, "z", 1), around(down_1, "z", -1)
    up_2, down_2, code_column = tied(up_2, down_2, code_column)
    code_column = code_column[:, :, :LANES]
    code_all = lax.all_gather(code_column, ("y", "c"), axis=0).reshape(
        EXPERTS, PADDED, LANES
    )
    near = (z + jnp.array(NEAR, jnp.int32) + PLANES) % PLANES
    out_hits = pair_hits(numbers, near.astype(jnp.int32), code_column)
    plane = ("y", "c", "tp")

    def exchanged(blocks):
        return lax.all_to_all(blocks, plane, split_axis=0, concat_axis=0, tiled=True)

    up_3, down_3 = around(up_2, "z", 1), around(down_2, "z", -1)
    far = [around(up_3[:64], "z", 1), around(down_3[64:], "z", -1)]
    outgoing = expand(out_hits, [state, up_1, down_1, up_2, down_2, up_3, down_3, *far])
    outgoing, wide_second, down_first = tied(outgoing, wide_second, down_first)
    down_second = lax.ppermute(down_first, PAIR, second_move)
    arrived = exchanged(outgoing)
    codes = chosen_rows(numbers, code_all)

    groups = jnp.arange(EXPERTS, dtype=jnp.int32)
    inverse = jnp.sum(
        jnp.where(group_order[None, :] == groups[:, None], groups[None, :], 0), axis=1
    )
    source = inverse.reshape(PLANES, PLANES).T
    source_z, source_column = source // PLANES, source % PLANES
    distance = (source_z - z + PLANES) % PLANES
    position = jnp.zeros_like(distance)
    for spot_here, near in enumerate(NEAR):
        position = jnp.where(distance == near % PLANES, spot_here, position)
    origin = (source_column * PLANES + position)[:, :, None] * QUARTER + jnp.arange(
        QUARTER, dtype=jnp.int32
    )
    mine = lax.dynamic_index_in_dim(source, column, 0, keepdims=False)
    back_hits = pair_hits(numbers, (mine % PLANES) * PLANES + mine // PLANES, code_all)
    codes, back_hits = tied(codes, back_hits)
    wide_parts, down_parts = (
        [
            own,
            first,
            other_own,
            second,
            lax.ppermute(first, PAIR, both),
            lax.ppermute(second, PAIR, to_home),
        ]
        for own, first, other_own, second in (
            (wide, wide_first, wide_other, wide_second),
            (down, down_first, down_other, down_second),
        )
    )
    result = expert(
        numbers,
        arrived.reshape(PLANES, TP, 64, COLS),
        codes,
        origin.reshape(512, 1),
        post_gain[None],
        router.T,
        wide_parts,
        down_parts,
    )
    answers = exchanged(result.reshape(32, 64, COLS))
    sums = combine(back_hits, answers).reshape(PLANES * ROWS, COLS)
    return lax.psum_scatter(sums, "z", scatter_dimension=0, tiled=True)


def solution(mesh):
    split = Mesh(mesh.devices.reshape(PLANES, 4, 2, TP), ("z", "y", "c", "tp"))
    req = ("z", "y", "c")
    return jax.shard_map(
        per_device,
        mesh=split,
        in_specs=(
            P(req, None, "tp"),
            P(req, None),
            P("tp"),
            P("tp"),
            P(req, None, None, "tp"),
            P(req, None, None, "tp"),
            P(req),
            P(req),
            P(),
            P(req, None),
            P("tp", None),
            P(),
            P(),
            P(req, None, "tp"),
            P(req, None, "tp"),
            P(req, "tp", None),
        ),
        out_specs=P(req, "tp"),
        check_vma=False,
    )
```

```python
import functools
import math

import jax
import jax.numpy as jnp
from jax import lax
from jax.experimental import pallas as pl
from jax.experimental.pallas import tpu as pltpu
from jax.sharding import Mesh, PartitionSpec as P

HEAD_DIM = 128
HEADS_HERE = 4
PRE = 128
DEC = 4
ROWS = PRE + DEC
PADDED = 136
SLOTS = 512
COLS = 512
FULL = 2048
EXPERTS = 64
LANES = 128
CAP = 32
PLANES = 8
TP = 4
QUARTER = 8
PAIR_LANES = 512
VMEM_LIMIT = 56 * 1024 * 1024
NEAR = (0, -1, 1, -2, 2, -3, 3, 4)
BF = jnp.bfloat16
F32 = jnp.float32
VM = pl.BlockSpec(memory_space=pltpu.VMEM)
SM = pl.BlockSpec(memory_space=pltpu.SMEM)
HB = pl.BlockSpec(memory_space=pl.ANY)


def dot(a, b, contract_a=1, contract_b=0):
    return lax.dot_general(
        a, b, (((contract_a,), (contract_b,)), ((), ())), preferred_element_type=F32
    )


def iota(shape, axis):
    return lax.broadcasted_iota(jnp.int32, shape, axis)


def attention_kernel(
    numbers, proj, inv, cosine, sine, q_gain, k_gain, context, cache, weight, own, *rest
):
    sends, total = rest[:3], rest[3]
    head = pl.program_id(0)
    factor = 1.0 / math.sqrt(HEAD_DIM)
    cos_v, sin_v = cosine[...], sine[...]

    def rotated(part, gain, column):
        norm = proj[part].astype(F32) * inv[:, column : column + 1] * gain[...]
        return (norm * cos_v + pltpu.roll(norm, HEAD_DIM // 2, 1) * sin_v).astype(BF)

    qr = rotated(0, q_gain, 0)
    kr = rotated(1, k_gain, 1)
    value = proj[2]
    low = jnp.finfo(F32).min

    q_pre, k_pre, v_pre = qr[:PRE], kr[:PRE], value[:PRE]
    rows = context.reshape(2 * SLOTS, HEAD_DIM)[...]
    column = iota((PRE, 2 * SLOTS), 1)
    seen = ((column & 1) == 0) & (column < 2 * numbers[0])
    s_old = jnp.where(seen, dot(q_pre, rows, 1, 1) * factor, low)
    causal = iota((PRE, PRE), 1) <= iota((PRE, PRE), 0)
    s_new = jnp.where(causal, dot(q_pre, k_pre, 1, 1) * factor, low)
    top = jnp.maximum(
        jnp.max(s_old, axis=1, keepdims=True), jnp.max(s_new, axis=1, keepdims=True)
    )
    e_old = jnp.where(seen, jnp.exp(s_old - top), 0.0)
    e_new = jnp.where(causal, jnp.exp(s_new - top), 0.0)
    share = 1.0 / (
        jnp.sum(e_old, axis=1, keepdims=True) + jnp.sum(e_new, axis=1, keepdims=True)
    )
    p_old = pltpu.roll(e_old * share, 1, 1).astype(BF)
    p_new = (e_new * share).astype(BF)
    mixed_pre = (dot(p_old, rows) + dot(p_new, v_pre)).astype(BF)

    q_dec, k_dec, v_dec = qr[PRE:], kr[PRE:], value[PRE:]
    keys = cache.reshape(DEC * 2 * SLOTS, HEAD_DIM)[...]
    row = iota((DEC, DEC * 2 * SLOTS), 0)
    column = iota((DEC, DEC * 2 * SLOTS), 1)
    length = jnp.where(
        row == 0,
        numbers[1],
        jnp.where(row == 1, numbers[2], jnp.where(row == 2, numbers[3], numbers[4])),
    )
    place = column - row * (2 * SLOTS)
    seen = ((column & 1) == 0) & (place >= 0) & (place < 2 * length)
    s_old = jnp.where(seen, dot(q_dec, keys, 1, 1) * factor, low)
    s_own = (
        jnp.sum(q_dec.astype(F32) * k_dec.astype(F32), axis=1, keepdims=True) * factor
    )
    top = jnp.maximum(jnp.max(s_old, axis=1, keepdims=True), s_own)
    e_old = jnp.where(seen, jnp.exp(s_old - top), 0.0)
    e_own = jnp.exp(s_own - top)
    share = 1.0 / (jnp.sum(e_old, axis=1, keepdims=True) + e_own)
    p_old = pltpu.roll(e_old * share, 1, 1).astype(BF)
    p_own = (e_own * share).astype(BF).astype(F32)
    mixed_dec = (dot(p_old, keys) + p_own * v_dec.astype(F32)).astype(BF)

    w = weight[...]
    out_pre = dot(mixed_pre, w)
    out_dec = dot(mixed_dec, w)

    @pl.when(head == 0)
    def _():
        for block in range(TP):
            span = slice(block * COLS, (block + 1) * COLS)
            total[block, :PRE] = out_pre[:, span]
            total[block, PRE:] = out_dec[:, span]

    @pl.when(head > 0)
    def _():
        for block in range(TP):
            span = slice(block * COLS, (block + 1) * COLS)
            total[block, :PRE] += out_pre[:, span]
            total[block, PRE:] += out_dec[:, span]

    @pl.when(head == HEADS_HERE - 1)
    def _():
        own[...] = total[numbers[5]]
        for step in range(1, TP):
            sends[step - 1][...] = total[(numbers[5] + step) % TP].astype(BF)


def attention(numbers, proj, inv, cosine, sine, q_gain, k_gain, context, cache, weight):
    whole = lambda *shape: pl.BlockSpec(shape, lambda h: (0,) * len(shape))
    return pl.pallas_call(
        attention_kernel,
        grid=(HEADS_HERE,),
        in_specs=[
            SM,
            pl.BlockSpec((3, ROWS, HEAD_DIM), lambda h: (0, 0, h)),
            whole(ROWS, 2),
            whole(ROWS, HEAD_DIM),
            whole(ROWS, HEAD_DIM),
            pl.BlockSpec((1, HEAD_DIM), lambda h: (0, h)),
            pl.BlockSpec((1, HEAD_DIM), lambda h: (0, h)),
            pl.BlockSpec((1, SLOTS, 2, HEAD_DIM), lambda h: (0, 0, 0, h)),
            pl.BlockSpec((DEC, SLOTS, 2, HEAD_DIM), lambda h: (0, 0, 0, h)),
            pl.BlockSpec((HEAD_DIM, FULL), lambda h: (h, 0)),
        ],
        out_specs=[whole(ROWS, COLS)] * TP,
        out_shape=[jax.ShapeDtypeStruct((ROWS, COLS), F32)]
        + [jax.ShapeDtypeStruct((ROWS, COLS), BF)] * (TP - 1),
        scratch_shapes=[pltpu.VMEM((TP, ROWS, COLS), F32)],
        compiler_params=pltpu.CompilerParams(vmem_limit_bytes=VMEM_LIMIT),
        cost_estimate=pl.CostEstimate(
            flops=2_000_000_000, bytes_accessed=10_000_000, transcendentals=1_000_000
        ),
        name="attention",
    )(numbers, proj, inv, cosine, sine, q_gain, k_gain, context, cache, weight)


def slot_part(code):
    wide = code.astype(F32)
    return jnp.where(wide > 64.0, wide - 64.0, wide)


def pair_onehot(code, plane, second):
    place = iota((LANES, PAIR_LANES), 1)
    device = place >> 4
    x, c, y = device & 3, (device >> 2) & 1, device >> 3
    expert = plane * PLANES + y * 2 + (x >> 1)
    spread = (iota((LANES, PAIR_LANES), 0) == expert).astype(F32).astype(BF)
    slot = dot(slot_part(code).astype(BF), spread)
    place = iota((1, PAIR_LANES), 1)
    device = place >> 4
    quarter = (device & 1) * 2 + ((device >> 2) & 1)
    wanted = quarter * QUARTER + (place & 7) + 1
    wanted = jnp.where(((place >> 3) & 1) == second, wanted, -1).astype(F32)
    return (slot == wanted).astype(F32).astype(BF)


def hits_kernel(numbers, order, code, out):
    for position in range(PLANES):
        out[position] = pair_onehot(
            code[order[position]][:ROWS], numbers[0], position & 1
        )


def pair_hits(numbers, order, code):
    return pl.pallas_call(
        hits_kernel,
        in_specs=[SM, SM, VM],
        out_specs=VM,
        out_shape=jax.ShapeDtypeStruct((PLANES, ROWS, PAIR_LANES), BF),
        compiler_params=pltpu.CompilerParams(vmem_limit_bytes=VMEM_LIMIT),
        cost_estimate=pl.CostEstimate(
            flops=700_000_000, bytes_accessed=4_000_000, transcendentals=0
        ),
        name="pair_hits",
    )(numbers, order, code)


def expand_kernel(hits, *refs):
    held, out = refs[:-1], refs[-1]
    for pair in range(PLANES // 2):
        filled = None
        for second in range(2):
            position = 2 * pair + second
            if position < PLANES - 1:
                rows = held[position][...]
            else:
                rows = jnp.concatenate(
                    [held[position][...], held[position + 1][...]], axis=0
                )
            part = dot(hits[position], rows, 0, 0)
            filled = part if filled is None else filled + part
        out[:, 16 * pair : 16 * pair + 16, :] = filled.astype(BF).reshape(32, 16, COLS)


def expand(hits, held):
    return pl.pallas_call(
        expand_kernel,
        in_specs=[VM] * (1 + len(held)),
        out_specs=VM,
        out_shape=jax.ShapeDtypeStruct((32, 64, COLS), BF),
        compiler_params=pltpu.CompilerParams(vmem_limit_bytes=VMEM_LIMIT),
        cost_estimate=pl.CostEstimate(
            flops=700_000_000, bytes_accessed=4_000_000, transcendentals=0
        ),
        name="expand",
    )(hits, *held)


def combine_kernel(hits, answers, out):
    rows = answers[...].reshape(PAIR_LANES, COLS)
    for second in range(2):
        out[second] = dot(hits[second], rows).astype(BF)


def combine(hits, answers):
    return pl.pallas_call(
        combine_kernel,
        grid=(PLANES // 2,),
        in_specs=[
            pl.BlockSpec((2, ROWS, PAIR_LANES), lambda p: (p, 0, 0)),
            pl.BlockSpec((32, 16, COLS), lambda p: (0, p, 0)),
        ],
        out_specs=pl.BlockSpec((2, ROWS, COLS), lambda p: (p, 0, 0)),
        out_shape=jax.ShapeDtypeStruct((PLANES, ROWS, COLS), BF),
        compiler_params=pltpu.CompilerParams(vmem_limit_bytes=VMEM_LIMIT),
        cost_estimate=pl.CostEstimate(
            flops=600_000_000, bytes_accessed=4_000_000, transcendentals=0
        ),
        name="combine",
    )(hits, answers)


def chosen_kernel(numbers, code, out):
    plane, expert, quarter = numbers[0], numbers[1], numbers[2]
    is_expert = iota((ROWS, LANES), 1) == expert
    place = iota((1, 64), 1)
    wanted = quarter * QUARTER + (place & 7) + 1

    def one(column, carry):
        filled = jnp.zeros((64, LANES), F32)
        for position in range(PLANES):
            z = (plane + NEAR[position] + PLANES) % PLANES
            rows = code[column * PLANES + z][:ROWS]
            slot = jnp.sum(
                jnp.where(is_expert, slot_part(rows), 0.0), axis=1, keepdims=True
            )
            aim = jnp.where((place >> 3) == position, wanted, -1).astype(F32)
            hits = (slot == aim).astype(F32).astype(BF)
            filled = filled + dot(hits, rows, 0, 0)
        out[column] = filled
        return carry

    lax.fori_loop(0, PLANES, one, 0)


def chosen_rows(numbers, code):
    return pl.pallas_call(
        chosen_kernel,
        in_specs=[SM, VM],
        out_specs=VM,
        out_shape=jax.ShapeDtypeStruct((PLANES, 64, LANES), F32),
        compiler_params=pltpu.CompilerParams(vmem_limit_bytes=VMEM_LIMIT),
        cost_estimate=pl.CostEstimate(
            flops=200_000_000, bytes_accessed=2_000_000, transcendentals=0
        ),
        name="chosen_rows",
    )(numbers, code)


def await_quarter(parts, target, sems, quarter):
    pltpu.make_async_copy(parts[1], target(None, quarter), sems.at[quarter]).wait()


def bring_quarters(parts, target, sems, at_home):
    own, first, other_own, second, other_first, other_second = parts
    def bring(source, quarter):
        pltpu.make_async_copy(
            target(source), target(None, quarter), sems.at[quarter]
        ).start()

    @pl.when(at_home == 1)
    def _():
        bring(own, 0)
        bring(other_second, 3)

    @pl.when(at_home == 0)
    def _():
        bring(other_own, 0)
        bring(second, 3)

    bring(first, 1)
    bring(other_first, 2)


def expert_kernel(numbers, arrived, codes, origin, gain, router, *refs):
    wide_parts, down_parts, out = refs[:6], refs[6:12], refs[12]
    wide, down, normed, hidden, sems = refs[13:18]
    at_home = numbers[3]
    to_wide = lambda source, quarter=None: wide.at[quarter] if source is None else source
    to_down = lambda source, quarter=None: (
        down.at[quarter * 256 : (quarter + 1) * 256] if source is None else source
    )
    bring_quarters(wide_parts, to_wide, sems.at[0], at_home)
    bring_quarters(down_parts, to_down, sems.at[1], at_home)

    squares = jnp.zeros((512, 1), F32)
    for x in range(TP):
        part = arrived[:, x].reshape(512, COLS).astype(F32)
        squares = squares + jnp.sum(part * part, axis=1, keepdims=True)
    scale = lax.rsqrt(squares / FULL + 1e-05)
    for x in range(TP):
        span = slice(x * COLS, (x + 1) * COLS)
        normed[:, span] = (arrived[:, x].reshape(512, COLS).astype(F32) * scale * gain[:, span]).astype(BF)
    logits = dot(normed[...], router[...], 1, 1)
    code = codes[...].reshape(512, LANES)[:, :EXPERTS]
    chosen = code > 0.0
    is_expert = iota((512, EXPERTS), 1) == numbers[1]
    top = jnp.max(jnp.where(chosen, logits, jnp.finfo(F32).min), axis=1, keepdims=True)
    raised = jnp.where(chosen, jnp.exp(jnp.minimum(logits - top, 0.0)), 0.0)
    bottom = jnp.sum(raised, axis=1, keepdims=True)
    share = jnp.sum(jnp.where(is_expert, raised, 0.0), axis=1, keepdims=True)
    gate = jnp.where(bottom > 0.0, share / jnp.where(bottom > 0.0, bottom, 1.0), 0.0)
    mark = jnp.sum(jnp.where(is_expert, code, 0.0), axis=1, keepdims=True)
    first_choice = (mark > 64.0).astype(F32)

    for quarter in (0, 3, 1, 2):
        await_quarter(wide_parts, to_wide, sems.at[0], quarter)
        gate_pre = dot(normed[...], wide[quarter, :FULL])
        up_pre = dot(normed[...], wide[quarter, FULL:])
        hidden[:, quarter * 256 : (quarter + 1) * 256] = (
            gate_pre / (1.0 + jnp.exp(-gate_pre)) * up_pre
        ).astype(BF)
    for quarter in range(4):
        await_quarter(down_parts, to_down, sems.at[1], quarter)
    move = (origin[...] == iota((512, 512), 1)).astype(F32).astype(BF)
    for x in range(TP):
        span = slice(x * COLS, (x + 1) * COLS)
        part = arrived[:, x].reshape(512, COLS).astype(F32)
        result = dot(hidden[...], down[:, span]).astype(BF).astype(F32) * gate
        piece = (result + first_choice * part).astype(BF)
        out[:, x] = dot(move, piece).astype(BF).reshape(PLANES, 64, COLS)


def expert(numbers, arrived, codes, origin, gain, router, wide_parts, down_parts):
    return pl.pallas_call(
        expert_kernel,
        in_specs=[SM] + [VM] * 5 + [HB] * 12,
        out_specs=VM,
        out_shape=jax.ShapeDtypeStruct((PLANES, TP, 64, COLS), BF),
        scratch_shapes=[
            pltpu.VMEM((4, 2 * FULL, 256), BF),
            pltpu.VMEM((1024, FULL), BF),
            pltpu.VMEM((512, FULL), BF),
            pltpu.VMEM((512, 1024), BF),
            pltpu.SemaphoreType.DMA((2, 4)),
        ],
        compiler_params=pltpu.CompilerParams(vmem_limit_bytes=VMEM_LIMIT),
        cost_estimate=pl.CostEstimate(
            flops=8_000_000_000, bytes_accessed=20_000_000, transcendentals=500_000
        ),
        name="expert",
    )(numbers, arrived, codes, origin, gain, router, *wide_parts, *down_parts)


def pair_moves():
    at = lambda core, x: core * TP + x
    over = lambda d: (d + TP) % (2 * TP)
    first = [
        (at(0, 0), at(0, 1)),
        (at(0, 1), at(0, 0)),
        (at(0, 2), at(1, 1)),
        (at(0, 3), at(1, 0)),
        (at(1, 2), at(1, 3)),
        (at(1, 3), at(1, 2)),
        (at(1, 1), at(0, 2)),
        (at(1, 0), at(0, 3)),
    ]
    second = [
        (at(1, 0), at(1, 1)),
        (at(1, 1), at(1, 0)),
        (at(0, 2), at(0, 3)),
        (at(0, 3), at(0, 2)),
    ]
    home = [at(0, 0), at(0, 1), at(1, 2), at(1, 3)]
    return (
        first,
        second,
        [(d, over(d)) for d in home],
        [(d, over(d)) for d in range(2 * TP)],
        [(over(d), d) for d in home],
    )


PAIR = ("c", "tp")


def tied(*values):
    return lax.optimization_barrier(values)


def around(value, axis, step):
    count = lax.axis_size(axis)
    return lax.ppermute(value, axis, [(i, (i + step) % count) for i in range(count)])


def per_device(
    projected,
    residual,
    query_gain,
    key_gain,
    context_cache,
    decode_cache,
    offsets,
    lengths,
    group_order,
    expert_ids,
    out_weight,
    post_gain,
    router,
    gate_weight,
    up_weight,
    down_weight,
):
    z, y, c, tp = (lax.axis_index(name) for name in ("z", "y", "c", "tp"))
    column = y * 2 + c

    every = jnp.arange(LANES, dtype=jnp.int32)
    chosen = jnp.zeros((ROWS, LANES), jnp.bool_)
    for k in range(expert_ids.shape[1]):
        chosen = chosen | (expert_ids[:, k : k + 1] == every[None, :])
    below = jnp.arange(ROWS)[:, None] >= jnp.arange(ROWS)[None, :]
    slot = dot(below.astype(BF), chosen.astype(BF))
    first_choice = expert_ids[:, :1] == every[None, :]
    code = jnp.where(chosen, slot + 64.0 * first_choice, 0.0).astype(BF)
    widened = jnp.pad(code, ((0, PADDED - ROWS), (0, COLS - LANES)))
    code_column = lax.all_gather(widened, "z", axis=0)

    first_move, second_move, out_of_home, both, to_home = pair_moves()
    wide = jnp.concatenate([gate_weight[0], up_weight[0]], axis=0)
    down = down_weight[0]

    proj = jnp.transpose(projected, (1, 0, 2))
    raw = proj[:2].astype(F32)
    squares = jnp.sum(raw * raw, axis=2)
    shared = [around(squares, "tp", step) for step in range(1, TP)]
    squares = squares + shared[0] + shared[1] + shared[2]
    squares, wide = tied(squares, wide)
    wide_first = lax.ppermute(wide, PAIR, first_move)
    inv = lax.rsqrt(squares / FULL + 1e-05).T
    spot = jnp.arange(ROWS, dtype=jnp.int32)
    positions = offsets[0] + spot
    for i in range(DEC):
        positions = jnp.where(spot == PRE + i, lengths[i], positions)
    half = HEAD_DIM // 2
    frequency = 10000.0 ** (-2.0 * jnp.arange(half, dtype=F32) / HEAD_DIM)
    angles = positions.astype(F32)[:, None] * frequency[None, :]
    cosine, sine = jnp.cos(angles), jnp.sin(angles)
    cosine = jnp.concatenate([cosine, cosine], axis=1)
    sine = jnp.concatenate([-sine, sine], axis=1)
    numbers = jnp.concatenate([offsets, lengths, tp[None].astype(jnp.int32)])
    own, *sends = attention(
        numbers,
        proj,
        inv,
        cosine,
        sine,
        query_gain[None],
        key_gain[None],
        context_cache,
        decode_cache,
        out_weight,
    )
    *sends, wide_first = tied(*sends, wide_first)
    state = own
    for step in range(1, TP):
        state = state + around(sends[step - 1], "tp", step).astype(F32)
    residual_here = lax.dynamic_slice_in_dim(residual, tp * COLS, COLS, 1)
    state = (residual_here.astype(F32) + state).astype(BF)
    serves = y * 2 + tp // 2
    quarter = (tp % 2) * 2 + c
    at_home = (tp // 2 == c).astype(jnp.int32)
    numbers = jnp.stack([z, z * PLANES + serves, quarter, at_home]).astype(jnp.int32)

    state, wide_first, down = tied(state, wide_first, down)
    down_first = lax.ppermute(down, PAIR, first_move)
    wide_second = lax.ppermute(wide_first, PAIR, second_move)

    up_1, down_1 = around(state, "z", 1), around(state, "z", -1)
    up_2, down_2 = around(up_1, "z", 1), around(down_1, "z", -1)
    up_2, down_2, code_column, down_first = tied(up_2, down_2, code_column, down_first)
    code_column = code_column[:, :, :LANES]
    code_all = lax.all_gather(code_column, ("y", "c"), axis=0).reshape(
        EXPERTS, PADDED, LANES
    )
    near = (z + jnp.array(NEAR, jnp.int32) + PLANES) % PLANES
    out_hits = pair_hits(numbers, near.astype(jnp.int32), code_column)
    plane = ("y", "c", "tp")

    def exchanged(blocks):
        return lax.all_to_all(blocks, plane, split_axis=0, concat_axis=0, tiled=True)

    up_3, down_3 = around(up_2, "z", 1), around(down_2, "z", -1)
    up_3, down_3, down_first = tied(up_3, down_3, down_first)
    down_second = lax.ppermute(down_first, PAIR, second_move)
    far = [around(up_3[:64], "z", 1), around(down_3[64:], "z", -1)]
    outgoing = expand(out_hits, [state, up_1, down_1, up_2, down_2, up_3, down_3, *far])
    outgoing, wide_second = tied(outgoing, wide_second)
    arrived = exchanged(outgoing)
    codes = chosen_rows(numbers, code_all)

    groups = jnp.arange(EXPERTS, dtype=jnp.int32)
    inverse = jnp.sum(
        jnp.where(group_order[None, :] == groups[:, None], groups[None, :], 0), axis=1
    )
    source = inverse.reshape(PLANES, PLANES).T
    source_z, source_column = source // PLANES, source % PLANES
    distance = (source_z - z + PLANES) % PLANES
    position = jnp.zeros_like(distance)
    for spot_here, near in enumerate(NEAR):
        position = jnp.where(distance == near % PLANES, spot_here, position)
    origin = (source_column * PLANES + position)[:, :, None] * QUARTER + jnp.arange(
        QUARTER, dtype=jnp.int32
    )
    mine = lax.dynamic_index_in_dim(source, column, 0, keepdims=False)
    back_hits = pair_hits(numbers, (mine % PLANES) * PLANES + mine // PLANES, code_all)
    codes, back_hits = tied(codes, back_hits)
    wide_parts, down_parts = (
        [
            own,
            first,
            lax.ppermute(own, PAIR, out_of_home),
            second,
            lax.ppermute(first, PAIR, both),
            lax.ppermute(second, PAIR, to_home),
        ]
        for own, first, second in (
            (wide, wide_first, wide_second),
            (down, down_first, down_second),
        )
    )
    result = expert(
        numbers,
        arrived.reshape(PLANES, TP, 64, COLS),
        codes,
        origin.reshape(512, 1),
        post_gain[None],
        router.T,
        wide_parts,
        down_parts,
    )
    answers = exchanged(result.reshape(32, 64, COLS))
    sums = combine(back_hits, answers).reshape(PLANES * ROWS, COLS)
    return lax.psum_scatter(sums, "z", scatter_dimension=0, tiled=True)


def solution(mesh):
    split = Mesh(mesh.devices.reshape(PLANES, 4, 2, TP), ("z", "y", "c", "tp"))
    req = ("z", "y", "c")
    return jax.shard_map(
        per_device,
        mesh=split,
        in_specs=(
            P(req, None, "tp"),
            P(req, None),
            P("tp"),
            P("tp"),
            P(req, None, None, "tp"),
            P(req, None, None, "tp"),
            P(req),
            P(req),
            P(),
            P(req, None),
            P("tp", None),
            P(),
            P(),
            P(req, None, "tp"),
            P(req, None, "tp"),
            P(req, "tp", None),
        ),
        out_specs=P(req, "tp"),
        check_vma=False,
    )
```

```python
import functools
import math

import jax
import jax.numpy as jnp
from jax import lax
from jax.experimental import pallas as pl
from jax.experimental.pallas import tpu as pltpu
from jax.sharding import Mesh, PartitionSpec as P

HEAD_DIM = 128
HEADS_HERE = 4
PRE = 128
DEC = 4
ROWS = PRE + DEC
PADDED = 136
SLOTS = 512
COLS = 512
FULL = 2048
EXPERTS = 64
LANES = 128
CAP = 32
PLANES = 8
TP = 4
QUARTER = 8
PAIR_LANES = 512
VMEM_LIMIT = 56 * 1024 * 1024
NEAR = (0, -1, 1, -2, 2, -3, 3, 4)
BF = jnp.bfloat16
F32 = jnp.float32
VM = pl.BlockSpec(memory_space=pltpu.VMEM)
SM = pl.BlockSpec(memory_space=pltpu.SMEM)
HB = pl.BlockSpec(memory_space=pl.ANY)


def dot(a, b, contract_a=1, contract_b=0):
    return lax.dot_general(
        a, b, (((contract_a,), (contract_b,)), ((), ())), preferred_element_type=F32
    )


def iota(shape, axis):
    return lax.broadcasted_iota(jnp.int32, shape, axis)


def attention_kernel(
    numbers, proj, inv, cosine, sine, q_gain, k_gain, context, cache, weight, own, *rest
):
    sends, total = rest[:3], rest[3]
    head = pl.program_id(0)
    factor = 1.0 / math.sqrt(HEAD_DIM)
    cos_v, sin_v = cosine[...], sine[...]

    def rotated(part, gain, column):
        norm = proj[part].astype(F32) * inv[:, column : column + 1] * gain[...]
        return (norm * cos_v + pltpu.roll(norm, HEAD_DIM // 2, 1) * sin_v).astype(BF)

    qr = rotated(0, q_gain, 0)
    kr = rotated(1, k_gain, 1)
    value = proj[2]
    low = jnp.finfo(F32).min

    q_pre, k_pre, v_pre = qr[:PRE], kr[:PRE], value[:PRE]
    rows = context.reshape(2 * SLOTS, HEAD_DIM)[...]
    column = iota((PRE, 2 * SLOTS), 1)
    seen = ((column & 1) == 0) & (column < 2 * numbers[0])
    s_old = jnp.where(seen, dot(q_pre, rows, 1, 1) * factor, low)
    causal = iota((PRE, PRE), 1) <= iota((PRE, PRE), 0)
    s_new = jnp.where(causal, dot(q_pre, k_pre, 1, 1) * factor, low)
    top = jnp.maximum(
        jnp.max(s_old, axis=1, keepdims=True), jnp.max(s_new, axis=1, keepdims=True)
    )
    e_old = jnp.where(seen, jnp.exp(s_old - top), 0.0)
    e_new = jnp.where(causal, jnp.exp(s_new - top), 0.0)
    share = 1.0 / (
        jnp.sum(e_old, axis=1, keepdims=True) + jnp.sum(e_new, axis=1, keepdims=True)
    )
    p_old = pltpu.roll(e_old * share, 1, 1).astype(BF)
    p_new = (e_new * share).astype(BF)
    mixed_pre = (dot(p_old, rows) + dot(p_new, v_pre)).astype(BF)

    q_dec, k_dec, v_dec = qr[PRE:], kr[PRE:], value[PRE:]
    keys = cache.reshape(DEC * 2 * SLOTS, HEAD_DIM)[...]
    row = iota((DEC, DEC * 2 * SLOTS), 0)
    column = iota((DEC, DEC * 2 * SLOTS), 1)
    length = jnp.where(
        row == 0,
        numbers[1],
        jnp.where(row == 1, numbers[2], jnp.where(row == 2, numbers[3], numbers[4])),
    )
    place = column - row * (2 * SLOTS)
    seen = ((column & 1) == 0) & (place >= 0) & (place < 2 * length)
    s_old = jnp.where(seen, dot(q_dec, keys, 1, 1) * factor, low)
    s_own = (
        jnp.sum(q_dec.astype(F32) * k_dec.astype(F32), axis=1, keepdims=True) * factor
    )
    top = jnp.maximum(jnp.max(s_old, axis=1, keepdims=True), s_own)
    e_old = jnp.where(seen, jnp.exp(s_old - top), 0.0)
    e_own = jnp.exp(s_own - top)
    share = 1.0 / (jnp.sum(e_old, axis=1, keepdims=True) + e_own)
    p_old = pltpu.roll(e_old * share, 1, 1).astype(BF)
    p_own = (e_own * share).astype(BF).astype(F32)
    mixed_dec = (dot(p_old, keys) + p_own * v_dec.astype(F32)).astype(BF)

    w = weight[...]
    out_pre = dot(mixed_pre, w)
    out_dec = dot(mixed_dec, w)

    @pl.when(head == 0)
    def _():
        for block in range(TP):
            span = slice(block * COLS, (block + 1) * COLS)
            total[block, :PRE] = out_pre[:, span]
            total[block, PRE:] = out_dec[:, span]

    @pl.when(head > 0)
    def _():
        for block in range(TP):
            span = slice(block * COLS, (block + 1) * COLS)
            total[block, :PRE] += out_pre[:, span]
            total[block, PRE:] += out_dec[:, span]

    @pl.when(head == HEADS_HERE - 1)
    def _():
        own[...] = total[numbers[5]]
        for step in range(1, TP):
            sends[step - 1][...] = total[(numbers[5] + step) % TP].astype(BF)


def attention(numbers, proj, inv, cosine, sine, q_gain, k_gain, context, cache, weight):
    whole = lambda *shape: pl.BlockSpec(shape, lambda h: (0,) * len(shape))
    return pl.pallas_call(
        attention_kernel,
        grid=(HEADS_HERE,),
        in_specs=[
            SM,
            pl.BlockSpec((3, ROWS, HEAD_DIM), lambda h: (0, 0, h)),
            whole(ROWS, 2),
            whole(ROWS, HEAD_DIM),
            whole(ROWS, HEAD_DIM),
            pl.BlockSpec((1, HEAD_DIM), lambda h: (0, h)),
            pl.BlockSpec((1, HEAD_DIM), lambda h: (0, h)),
            pl.BlockSpec((1, SLOTS, 2, HEAD_DIM), lambda h: (0, 0, 0, h)),
            pl.BlockSpec((DEC, SLOTS, 2, HEAD_DIM), lambda h: (0, 0, 0, h)),
            pl.BlockSpec((HEAD_DIM, FULL), lambda h: (h, 0)),
        ],
        out_specs=[whole(ROWS, COLS)] * TP,
        out_shape=[jax.ShapeDtypeStruct((ROWS, COLS), F32)]
        + [jax.ShapeDtypeStruct((ROWS, COLS), BF)] * (TP - 1),
        scratch_shapes=[pltpu.VMEM((TP, ROWS, COLS), F32)],
        compiler_params=pltpu.CompilerParams(vmem_limit_bytes=VMEM_LIMIT),
        cost_estimate=pl.CostEstimate(
            flops=2_000_000_000, bytes_accessed=10_000_000, transcendentals=1_000_000
        ),
        name="attention",
    )(numbers, proj, inv, cosine, sine, q_gain, k_gain, context, cache, weight)


def slot_part(code):
    wide = code.astype(F32)
    return jnp.where(wide > 64.0, wide - 64.0, wide)


def pair_onehot(code, plane, second):
    place = iota((LANES, PAIR_LANES), 1)
    device = place >> 4
    x, c, y = device & 3, (device >> 2) & 1, device >> 3
    expert = plane * PLANES + y * 2 + (x >> 1)
    spread = (iota((LANES, PAIR_LANES), 0) == expert).astype(F32).astype(BF)
    slot = dot(slot_part(code).astype(BF), spread)
    place = iota((1, PAIR_LANES), 1)
    device = place >> 4
    quarter = (device & 1) * 2 + ((device >> 2) & 1)
    wanted = quarter * QUARTER + (place & 7) + 1
    wanted = jnp.where(((place >> 3) & 1) == second, wanted, -1).astype(F32)
    return (slot == wanted).astype(F32).astype(BF)


def hits_kernel(numbers, order, code, out):
    for position in range(PLANES):
        out[position] = pair_onehot(
            code[order[position]][:ROWS], numbers[0], position & 1
        )


def pair_hits(numbers, order, code):
    return pl.pallas_call(
        hits_kernel,
        in_specs=[SM, SM, VM],
        out_specs=VM,
        out_shape=jax.ShapeDtypeStruct((PLANES, ROWS, PAIR_LANES), BF),
        compiler_params=pltpu.CompilerParams(vmem_limit_bytes=VMEM_LIMIT),
        cost_estimate=pl.CostEstimate(
            flops=700_000_000, bytes_accessed=4_000_000, transcendentals=0
        ),
        name="pair_hits",
    )(numbers, order, code)


def expand_kernel(hits, *refs):
    held, out = refs[:-1], refs[-1]
    for pair in range(PLANES // 2):
        filled = None
        for second in range(2):
            position = 2 * pair + second
            if position < PLANES - 1:
                rows = held[position][...]
            else:
                rows = jnp.concatenate(
                    [held[position][...], held[position + 1][...]], axis=0
                )
            part = dot(hits[position], rows, 0, 0)
            filled = part if filled is None else filled + part
        out[:, 16 * pair : 16 * pair + 16, :] = filled.astype(BF).reshape(32, 16, COLS)


def expand(hits, held):
    return pl.pallas_call(
        expand_kernel,
        in_specs=[VM] * (1 + len(held)),
        out_specs=VM,
        out_shape=jax.ShapeDtypeStruct((32, 64, COLS), BF),
        compiler_params=pltpu.CompilerParams(vmem_limit_bytes=VMEM_LIMIT),
        cost_estimate=pl.CostEstimate(
            flops=700_000_000, bytes_accessed=4_000_000, transcendentals=0
        ),
        name="expand",
    )(hits, *held)


def combine_kernel(hits, answers, out):
    rows = answers[...].reshape(PAIR_LANES, COLS)
    for second in range(2):
        out[second] = dot(hits[second], rows).astype(BF)


def combine(hits, answers):
    return pl.pallas_call(
        combine_kernel,
        grid=(PLANES // 2,),
        in_specs=[
            pl.BlockSpec((2, ROWS, PAIR_LANES), lambda p: (p, 0, 0)),
            pl.BlockSpec((32, 16, COLS), lambda p: (0, p, 0)),
        ],
        out_specs=pl.BlockSpec((2, ROWS, COLS), lambda p: (p, 0, 0)),
        out_shape=jax.ShapeDtypeStruct((PLANES, ROWS, COLS), BF),
        compiler_params=pltpu.CompilerParams(vmem_limit_bytes=VMEM_LIMIT),
        cost_estimate=pl.CostEstimate(
            flops=600_000_000, bytes_accessed=4_000_000, transcendentals=0
        ),
        name="combine",
    )(hits, answers)


def chosen_kernel(numbers, code, out):
    plane, expert, quarter = numbers[0], numbers[1], numbers[2]
    is_expert = iota((ROWS, LANES), 1) == expert
    place = iota((1, 64), 1)
    wanted = quarter * QUARTER + (place & 7) + 1

    def one(column, carry):
        filled = jnp.zeros((64, LANES), F32)
        for position in range(PLANES):
            z = (plane + NEAR[position] + PLANES) % PLANES
            rows = code[column * PLANES + z][:ROWS]
            slot = jnp.sum(
                jnp.where(is_expert, slot_part(rows), 0.0), axis=1, keepdims=True
            )
            aim = jnp.where((place >> 3) == position, wanted, -1).astype(F32)
            hits = (slot == aim).astype(F32).astype(BF)
            filled = filled + dot(hits, rows, 0, 0)
        out[column] = filled
        return carry

    lax.fori_loop(0, PLANES, one, 0)


def chosen_rows(numbers, code):
    return pl.pallas_call(
        chosen_kernel,
        in_specs=[SM, VM],
        out_specs=VM,
        out_shape=jax.ShapeDtypeStruct((PLANES, 64, LANES), F32),
        compiler_params=pltpu.CompilerParams(vmem_limit_bytes=VMEM_LIMIT),
        cost_estimate=pl.CostEstimate(
            flops=200_000_000, bytes_accessed=2_000_000, transcendentals=0
        ),
        name="chosen_rows",
    )(numbers, code)


def await_quarter(parts, target, sems, quarter):
    pltpu.make_async_copy(parts[1], target(None, quarter), sems.at[quarter]).wait()


def bring_quarters(parts, target, sems, at_home):
    own, first, other_own, second, other_first, other_second = parts
    def bring(source, quarter):
        pltpu.make_async_copy(
            target(source), target(None, quarter), sems.at[quarter]
        ).start()

    @pl.when(at_home == 1)
    def _():
        bring(own, 0)
        bring(other_second, 3)

    @pl.when(at_home == 0)
    def _():
        bring(other_own, 0)
        bring(second, 3)

    bring(first, 1)
    bring(other_first, 2)


def expert_kernel(numbers, arrived, codes, origin, gain, router, *refs):
    wide_parts, down_parts, out = refs[:6], refs[6:12], refs[12]
    wide, down, normed, hidden, sems = refs[13:18]
    at_home = numbers[3]
    to_wide = lambda source, quarter=None: wide.at[quarter] if source is None else source
    to_down = lambda source, quarter=None: (
        down.at[quarter * 256 : (quarter + 1) * 256] if source is None else source
    )
    bring_quarters(wide_parts, to_wide, sems.at[0], at_home)
    bring_quarters(down_parts, to_down, sems.at[1], at_home)

    squares = jnp.zeros((512, 1), F32)
    for x in range(TP):
        part = arrived[:, x].reshape(512, COLS).astype(F32)
        squares = squares + jnp.sum(part * part, axis=1, keepdims=True)
    scale = lax.rsqrt(squares / FULL + 1e-05)
    for x in range(TP):
        span = slice(x * COLS, (x + 1) * COLS)
        normed[:, span] = (arrived[:, x].reshape(512, COLS).astype(F32) * scale * gain[:, span]).astype(BF)
    logits = dot(normed[...], router[...], 1, 1)
    code = codes[...].reshape(512, LANES)[:, :EXPERTS]
    chosen = code > 0.0
    is_expert = iota((512, EXPERTS), 1) == numbers[1]
    top = jnp.max(jnp.where(chosen, logits, jnp.finfo(F32).min), axis=1, keepdims=True)
    raised = jnp.where(chosen, jnp.exp(jnp.minimum(logits - top, 0.0)), 0.0)
    bottom = jnp.sum(raised, axis=1, keepdims=True)
    share = jnp.sum(jnp.where(is_expert, raised, 0.0), axis=1, keepdims=True)
    gate = jnp.where(bottom > 0.0, share / jnp.where(bottom > 0.0, bottom, 1.0), 0.0)
    mark = jnp.sum(jnp.where(is_expert, code, 0.0), axis=1, keepdims=True)
    first_choice = (mark > 64.0).astype(F32)

    for quarter in (0, 3, 1, 2):
        await_quarter(wide_parts, to_wide, sems.at[0], quarter)
        gate_pre = dot(normed[...], wide[quarter, :FULL])
        up_pre = dot(normed[...], wide[quarter, FULL:])
        hidden[:, quarter * 256 : (quarter + 1) * 256] = (
            gate_pre / (1.0 + jnp.exp(-gate_pre)) * up_pre
        ).astype(BF)
    for quarter in range(4):
        await_quarter(down_parts, to_down, sems.at[1], quarter)
    move = (origin[...] == iota((512, 512), 1)).astype(F32).astype(BF)
    for x in range(TP):
        span = slice(x * COLS, (x + 1) * COLS)
        part = arrived[:, x].reshape(512, COLS).astype(F32)
        result = dot(hidden[...], down[:, span]).astype(BF).astype(F32) * gate
        piece = (result + first_choice * part).astype(BF)
        out[:, x] = dot(move, piece).astype(BF).reshape(PLANES, 64, COLS)


def expert(numbers, arrived, codes, origin, gain, router, wide_parts, down_parts):
    return pl.pallas_call(
        expert_kernel,
        in_specs=[SM] + [VM] * 5 + [HB] * 12,
        out_specs=VM,
        out_shape=jax.ShapeDtypeStruct((PLANES, TP, 64, COLS), BF),
        scratch_shapes=[
            pltpu.VMEM((4, 2 * FULL, 256), BF),
            pltpu.VMEM((1024, FULL), BF),
            pltpu.VMEM((512, FULL), BF),
            pltpu.VMEM((512, 1024), BF),
            pltpu.SemaphoreType.DMA((2, 4)),
        ],
        compiler_params=pltpu.CompilerParams(vmem_limit_bytes=VMEM_LIMIT),
        cost_estimate=pl.CostEstimate(
            flops=8_000_000_000, bytes_accessed=20_000_000, transcendentals=500_000
        ),
        name="expert",
    )(numbers, arrived, codes, origin, gain, router, *wide_parts, *down_parts)


def pair_moves():
    at = lambda core, x: core * TP + x
    over = lambda d: (d + TP) % (2 * TP)
    first = [
        (at(0, 0), at(0, 1)),
        (at(0, 1), at(0, 0)),
        (at(0, 2), at(1, 1)),
        (at(0, 3), at(1, 0)),
        (at(1, 2), at(1, 3)),
        (at(1, 3), at(1, 2)),
        (at(1, 1), at(0, 2)),
        (at(1, 0), at(0, 3)),
    ]
    second = [
        (at(1, 0), at(1, 1)),
        (at(1, 1), at(1, 0)),
        (at(0, 2), at(0, 3)),
        (at(0, 3), at(0, 2)),
    ]
    home = [at(0, 0), at(0, 1), at(1, 2), at(1, 3)]
    return (
        first,
        second,
        [(d, over(d)) for d in home],
        [(d, over(d)) for d in range(2 * TP)],
        [(over(d), d) for d in home],
    )


PAIR = ("c", "tp")


def tied(*values):
    return lax.optimization_barrier(values)


def around(value, axis, step):
    count = lax.axis_size(axis)
    return lax.ppermute(value, axis, [(i, (i + step) % count) for i in range(count)])


def per_device(
    projected,
    residual,
    query_gain,
    key_gain,
    context_cache,
    decode_cache,
    offsets,
    lengths,
    group_order,
    expert_ids,
    out_weight,
    post_gain,
    router,
    gate_weight,
    up_weight,
    down_weight,
):
    z, y, c, tp = (lax.axis_index(name) for name in ("z", "y", "c", "tp"))
    column = y * 2 + c

    every = jnp.arange(LANES, dtype=jnp.int32)
    chosen = jnp.zeros((ROWS, LANES), jnp.bool_)
    for k in range(expert_ids.shape[1]):
        chosen = chosen | (expert_ids[:, k : k + 1] == every[None, :])
    below = jnp.arange(ROWS)[:, None] >= jnp.arange(ROWS)[None, :]
    slot = dot(below.astype(BF), chosen.astype(BF))
    first_choice = expert_ids[:, :1] == every[None, :]
    code = jnp.where(chosen, slot + 64.0 * first_choice, 0.0).astype(BF)
    widened = jnp.pad(code, ((0, PADDED - ROWS), (0, COLS - LANES)))
    code_column = lax.all_gather(widened, "z", axis=0)

    first_move, second_move, out_of_home, both, to_home = pair_moves()
    wide = jnp.concatenate([gate_weight[0], up_weight[0]], axis=0)
    down = down_weight[0]

    proj = jnp.transpose(projected, (1, 0, 2))
    raw = proj[:2].astype(F32)
    squares = jnp.sum(raw * raw, axis=2)
    shared = [around(squares, "tp", step) for step in range(1, TP)]
    squares = squares + shared[0] + shared[1] + shared[2]
    squares, wide = tied(squares, wide)
    wide_first = lax.ppermute(wide, PAIR, first_move)
    inv = lax.rsqrt(squares / FULL + 1e-05).T
    spot = jnp.arange(ROWS, dtype=jnp.int32)
    positions = offsets[0] + spot
    for i in range(DEC):
        positions = jnp.where(spot == PRE + i, lengths[i], positions)
    half = HEAD_DIM // 2
    frequency = 10000.0 ** (-2.0 * jnp.arange(half, dtype=F32) / HEAD_DIM)
    angles = positions.astype(F32)[:, None] * frequency[None, :]
    cosine, sine = jnp.cos(angles), jnp.sin(angles)
    cosine = jnp.concatenate([cosine, cosine], axis=1)
    sine = jnp.concatenate([-sine, sine], axis=1)
    numbers = jnp.concatenate([offsets, lengths, tp[None].astype(jnp.int32)])
    own, *sends = attention(
        numbers,
        proj,
        inv,
        cosine,
        sine,
        query_gain[None],
        key_gain[None],
        context_cache,
        decode_cache,
        out_weight,
    )
    *sends, wide_first = tied(*sends, wide_first)
    state = own
    for step in range(1, TP):
        state = state + around(sends[step - 1], "tp", step).astype(F32)
    residual_here = lax.dynamic_slice_in_dim(residual, tp * COLS, COLS, 1)
    state = (residual_here.astype(F32) + state).astype(BF)
    serves = y * 2 + tp // 2
    quarter = (tp % 2) * 2 + c
    at_home = (tp // 2 == c).astype(jnp.int32)
    numbers = jnp.stack([z, z * PLANES + serves, quarter, at_home]).astype(jnp.int32)

    state, wide_first, down = tied(state, wide_first, down)
    down_first = lax.ppermute(down, PAIR, first_move)
    wide_second = lax.ppermute(wide_first, PAIR, second_move)

    up_1, down_1 = around(state, "z", 1), around(state, "z", -1)
    up_2, down_2 = around(up_1, "z", 1), around(down_1, "z", -1)
    up_2, down_2, code_column = tied(up_2, down_2, code_column)
    code_column = code_column[:, :, :LANES]
    code_all = lax.all_gather(code_column, ("y", "c"), axis=0).reshape(
        EXPERTS, PADDED, LANES
    )
    near = (z + jnp.array(NEAR, jnp.int32) + PLANES) % PLANES
    out_hits = pair_hits(numbers, near.astype(jnp.int32), code_column)
    plane = ("y", "c", "tp")

    def exchanged(blocks):
        return lax.all_to_all(blocks, plane, split_axis=0, concat_axis=0, tiled=True)

    up_3, down_3 = around(up_2, "z", 1), around(down_2, "z", -1)
    far = [around(up_3[:64], "z", 1), around(down_3[64:], "z", -1)]
    outgoing = expand(out_hits, [state, up_1, down_1, up_2, down_2, up_3, down_3, *far])
    outgoing, wide_second, down_first = tied(outgoing, wide_second, down_first)
    down_second = lax.ppermute(down_first, PAIR, second_move)
    arrived = exchanged(outgoing)
    codes = chosen_rows(numbers, code_all)

    groups = jnp.arange(EXPERTS, dtype=jnp.int32)
    inverse = jnp.sum(
        jnp.where(group_order[None, :] == groups[:, None], groups[None, :], 0), axis=1
    )
    source = inverse.reshape(PLANES, PLANES).T
    source_z, source_column = source // PLANES, source % PLANES
    distance = (source_z - z + PLANES) % PLANES
    position = jnp.zeros_like(distance)
    for spot_here, near in enumerate(NEAR):
        position = jnp.where(distance == near % PLANES, spot_here, position)
    origin = (source_column * PLANES + position)[:, :, None] * QUARTER + jnp.arange(
        QUARTER, dtype=jnp.int32
    )
    mine = lax.dynamic_index_in_dim(source, column, 0, keepdims=False)
    back_hits = pair_hits(numbers, (mine % PLANES) * PLANES + mine // PLANES, code_all)
    codes, back_hits = tied(codes, back_hits)
    wide_parts, down_parts = (
        [
            own,
            first,
            lax.ppermute(own, PAIR, out_of_home),
            second,
            lax.ppermute(first, PAIR, both),
            lax.ppermute(second, PAIR, to_home),
        ]
        for own, first, second in (
            (wide, wide_first, wide_second),
            (down, down_first, down_second),
        )
    )
    result = expert(
        numbers,
        arrived.reshape(PLANES, TP, 64, COLS),
        codes,
        origin.reshape(512, 1),
        post_gain[None],
        router.T,
        wide_parts,
        down_parts,
    )
    answers = exchanged(result.reshape(32, 64, COLS))
    sums = combine(back_hits, answers).reshape(PLANES * ROWS, COLS)
    return lax.psum_scatter(sums, "z", scatter_dimension=0, tiled=True)


def solution(mesh):
    split = Mesh(mesh.devices.reshape(PLANES, 4, 2, TP), ("z", "y", "c", "tp"))
    req = ("z", "y", "c")
    return jax.shard_map(
        per_device,
        mesh=split,
        in_specs=(
            P(req, None, "tp"),
            P(req, None),
            P("tp"),
            P("tp"),
            P(req, None, None, "tp"),
            P(req, None, None, "tp"),
            P(req),
            P(req),
            P(),
            P(req, None),
            P("tp", None),
            P(),
            P(),
            P(req, None, "tp"),
            P(req, None, "tp"),
            P(req, "tp", None),
        ),
        out_specs=P(req, "tp"),
        check_vma=False,
    )
```
